32 devices in a mesh: section: 2 (over core), ctx: 4 (over z), fsdp: 4 (over y, x).
Axes of the slice: x: 2, y: 2, z: 4, core: 2. Of those that a mesh axis runs over, the one named last changes fastest.
Arguments:
- inputs: bfloat16 [2, 4, 1024, 768], P(None, 'fsdp', 'ctx'), may hold values from -6 to 6
- cotangent: bfloat16 [2, 4, 1024, 768], P(None, 'fsdp', 'ctx'), may hold values from -6 to 6
- block_order: int32 [4], replicated, may hold values from 0 to 3, as said below
- norm_gain: float32 [2, 2, 768], P('section', None, 'fsdp'), may hold values from 0.5 to 1.5
- norm_bias: float32 [2, 2, 768], P('section', None, 'fsdp'), may hold values from -2 to 2
- qkv_weight: bfloat16 [2, 768, 2304], P('section', 'fsdp'), may hold values from -0.21875 to 0.21875
- biases: float32 [2, 6912], P('section', 'fsdp'), may hold values from -2 to 2
- out_weight: bfloat16 [2, 768, 768], P('section', 'fsdp'), may hold values from -0.875 to 0.875
- up_weight: bfloat16 [2, 768, 3072], P('section', 'fsdp'), may hold values from -0.21875 to 0.21875
- down_weight: bfloat16 [2, 3072, 768], P('section', 'fsdp'), may hold values from -0.109375 to 0.109375
Outputs:
- layer_out: bfloat16 [2, 2, 4, 1024, 768], P('section', None, 'fsdp', 'ctx')
- input_grads: bfloat16 [2, 2, 4, 1024, 768], P('section', None, 'fsdp', 'ctx')
- gain_grads: float32 [2, 2, 768], P('section', None, ('ctx', 'fsdp'))
- shift_grads: float32 [2, 2, 768], P('section', None, ('ctx', 'fsdp'))
- qkv_grads: float32 [2, 768, 2304], P('section', ('ctx', 'fsdp'))
- bias_grads: float32 [2, 6912], P('section', ('ctx', 'fsdp'))
- out_grads: float32 [2, 768, 768], P('section', ('ctx', 'fsdp'))
- up_grads: float32 [2, 768, 3072], P('section', ('ctx', 'fsdp'))
- down_grads: float32 [2, 3072, 768], P('section', ('ctx', 'fsdp'))
The draws below stay inside these ranges and needn't reach their ends.
Inputs may be any that keep to these rules, and one draw needn't show every extreme that they name: block_order is a permutation of 0 to 3.
All inputs are finite; a program needn't handle non-finite values.
Results may differ from the reference program's by a relative error of at most 0.028.
Values may be sent and summed in bfloat16 or wider, within the bound.
No kernel may reach another device: no remote copies, remote signals or barrier semaphores. Data moves between devices by JAX's collectives and lax.ppermute only.
A program may use at most 256 MiB of HBM per device.

```python
import jax
import jax.numpy as jnp
from jax import lax

D = 768
HEADS = 12
HEAD_DIM = 64
ROT = 16
FF = 3072
LEN = 1024
MICRO = 2
LAYERS = 2
RANKS = 4
SEQS = 4
BIAS = 6912


def draw_block_order(key, part):
    key = jax.random.fold_in(key, 7)
    return jax.random.permutation(key, RANKS).astype(jnp.int32)


def shard_levels(stream_key, shape, shards, low, top_value):
    level, own = 1.0, jax.random.fold_in(stream_key, 6)
    for dim, shards_of in shards:
        steps = jnp.exp(jax.random.uniform(jax.random.fold_in(own, dim), (shards_of,), jnp.float32, low / len(shards), top_value / len(shards)))
        level = level * jnp.repeat(steps, shape[dim] // shards_of).reshape([-1 if axis == dim else 1 for axis in range(len(shape))])
    return level


def scatter_about(key, dims, deviation, bound, cuts=(), held_as=jnp.bfloat16):
    values = jax.random.normal(key, dims, jnp.float32) * deviation
    if len(cuts) > 0:
        values = shard_levels(key, dims, cuts, -0.22, 0.18) * values
    return jnp.clip(values, min=-bound, max=bound).astype(held_as)


def setup_inputs(seed: int = 0) -> dict:
    seeds = jax.random.split(jax.random.key(seed), 11)
    inputs = scatter_about(seeds[0], (MICRO, SEQS, LEN, D), 1.0, 6.0, ((1, 4), (2, 4)))
    cotangent = scatter_about(seeds[1], (MICRO, SEQS, LEN, D), 1.0, 6.0, ((1, 4), (2, 4)))
    block_order = draw_block_order(jax.random.fold_in(seeds[10], 71), 0)
    norm_gain = jnp.clip(1.0 + 0.1 * jax.random.normal(seeds[3], (LAYERS, 2, D), jnp.float32), 0.5, 1.5)
    norm_bias = scatter_about(seeds[4], (LAYERS, 2, D), 0.3, 2.0, ((0, 2), (2, 4)), jnp.float32)
    qkv_weight = scatter_about(seeds[5], (LAYERS, D, 3 * D), D ** -0.5, 0.21875, ((0, 2), (1, 4)))
    biases = scatter_about(seeds[6], (LAYERS, BIAS), 0.3, 2.0, ((0, 2), (1, 4)), jnp.float32)
    out_weight = scatter_about(seeds[7], (LAYERS, D, D), (D // 16) ** -0.5, 0.875, ((0, 2), (1, 4)))
    up_weight = scatter_about(seeds[8], (LAYERS, D, FF), D ** -0.5, 0.21875, ((0, 2), (1, 4)))
    down_weight = scatter_about(seeds[9], (LAYERS, FF, D), FF ** -0.5, 0.109375, ((0, 2), (1, 4)))
    return {"inputs": inputs, "cotangent": cotangent, "block_order": block_order, "norm_gain": norm_gain, "norm_bias": norm_bias, "qkv_weight": qkv_weight, "biases": biases, "out_weight": out_weight, "up_weight": up_weight, "down_weight": down_weight}


@jax.custom_vjp
def low(v):
    return lax.optimization_barrier(v.astype(jnp.bfloat16)).astype(jnp.float32)

@jax.custom_vjp
def low_back(v):
    return v

def low_keep(v):
    return (low(v), None)

def low_pass(kept, grad):
    return (grad,)

def back_keep(v):
    return (v, None)

def back_low(kept, grad):
    return (low(grad),)
low.defvjp(low_keep, low_pass)
low_back.defvjp(back_keep, back_low)

def highest_dot(left, right):
    return jnp.dot(left, right, precision=lax.Precision.HIGHEST)

def norm_apply(tok_rows, gain_vec, shift_vec):
    row_mean = lax.optimization_barrier(jnp.mean(tok_rows, -1, keepdims=True))
    centred = tok_rows - row_mean
    spread = lax.optimization_barrier(jnp.mean(centred * centred, -1, keepdims=True))
    return centred * lax.rsqrt(spread + 1e-05) * gain_vec + shift_vec

def angle_tables(places):
    half_dims = ROT // 2
    frequency = 10000.0 ** (-(jnp.arange(half_dims, dtype=jnp.float32) * 2.0) / ROT)
    phases = places.astype(jnp.float32)[:, None] * frequency[None, :]
    phases = jnp.concatenate([phases, phases], -1)
    return (jnp.cos(phases)[:, None, :], jnp.sin(phases)[:, None, :])

def rotary(head_rows, cosine, sine):
    half_dims = ROT // 2
    rot_part = head_rows[..., :ROT]
    swapped = jnp.concatenate([-rot_part[..., half_dims:], rot_part[..., :half_dims]], -1)
    return jnp.concatenate([rot_part * cosine + swapped * sine, head_rows[..., ROT:]], -1)

def token_places(block_order):
    block_rows = LEN // (2 * RANKS)
    row_ids = jnp.arange(LEN, dtype=jnp.int32)
    owner_ids = row_ids // (2 * block_rows)
    within = row_ids % (2 * block_rows)
    first_block = block_order[owner_ids]
    block_ids = jnp.where(within < block_rows, first_block, 2 * RANKS - 1 - first_block)
    return (block_ids * block_rows + within % block_rows).astype(jnp.int32)

def layer_apply(tok_rows, params, cosine, sine, places):
    gain_pair, shift_pair, qkv_mat, bias_vec, out_mat, up_mat, down_mat = params
    attn_in = low(norm_apply(tok_rows, gain_pair[0], shift_pair[0]))
    mlp_in = low(norm_apply(tok_rows, gain_pair[1], shift_pair[1]))
    qkv_rows = low_back(highest_dot(attn_in, qkv_mat) + bias_vec[:3 * D]).reshape(LEN, 3, HEADS, HEAD_DIM)
    query_rows = low(rotary(qkv_rows[:, 0], cosine, sine))
    key_rows = low(rotary(qkv_rows[:, 1], cosine, sine))
    value_rows = low(qkv_rows[:, 2])
    block_size = min(512, LEN)

    def attend(pair_in):
        query_block, place_block = pair_in
        scores = low_back(jnp.einsum('qhd,khd->hqk', query_block, key_rows, precision=lax.Precision.HIGHEST) * 0.125)
        scores = jnp.where(place_block[None, :, None] >= places[None, None, :], scores, -1e+30)
        row_max = lax.optimization_barrier(jnp.max(scores, -1, keepdims=True))
        exp_scores = jnp.exp(scores - row_max)
        prob_rows = exp_scores / lax.optimization_barrier(jnp.sum(exp_scores, -1, keepdims=True))
        return jnp.einsum('hqk,khd->qhd', low(prob_rows), value_rows, precision=lax.Precision.HIGHEST)
    mixed_rows = lax.map(jax.checkpoint(attend), (query_rows.reshape(LEN // block_size, block_size, HEADS, HEAD_DIM), places.reshape(LEN // block_size, block_size)))
    mixed_rows = low_back(low(mixed_rows.reshape(LEN, D)))
    attn_rows = highest_dot(mixed_rows, out_mat) + bias_vec[3 * D:4 * D]
    up_rows = low_back(highest_dot(mlp_in, up_mat) + bias_vec[4 * D:4 * D + FF])
    gelu_rows = low(jax.nn.gelu(up_rows, approximate=False))
    mlp_rows = highest_dot(gelu_rows, down_mat) + bias_vec[4 * D + FF:]
    return tok_rows + low_back(attn_rows + mlp_rows)

def reference(inputs, cotangent, block_order, norm_gain, norm_bias, qkv_weight, biases, out_weight, up_weight, down_weight):
    places = token_places(block_order)
    cosine, sine = angle_tables(places)
    tok_all = inputs.astype(jnp.float32).reshape(MICRO * SEQS, LEN, D)
    mid_zero = jnp.zeros_like(tok_all)

    def forward(tok_in, mid_in, gain_all, shift_all, qkv_all, bias_all, out_all, up_all, down_all):

        def params_of(layer_idx):
            return (gain_all[layer_idx], shift_all[layer_idx], qkv_all[layer_idx], bias_all[layer_idx], out_all[layer_idx], up_all[layer_idx], down_all[layer_idx])

        def sequence_step(carry_val, pair_in):
            tok_rows, extra_in = pair_in
            first_out = low(layer_apply(tok_rows, params_of(0), cosine, sine, places))
            second_out = layer_apply(low_back(first_out + extra_in), params_of(1), cosine, sine, places)
            return (carry_val, (first_out, second_out))
        carry_val, outs_pair = lax.scan(jax.checkpoint(sequence_step), jnp.zeros((), jnp.float32), (tok_in, mid_in))
        return outs_pair
    (firsts, seconds), pullback = jax.vjp(forward, tok_all, mid_zero, norm_gain.astype(jnp.float32), norm_bias.astype(jnp.float32), qkv_weight.astype(jnp.float32), biases.astype(jnp.float32), out_weight.astype(jnp.float32), up_weight.astype(jnp.float32), down_weight.astype(jnp.float32))
    gradients = pullback((jnp.zeros_like(firsts), cotangent.astype(jnp.float32).reshape(MICRO * SEQS, LEN, D)))
    shape_out = (MICRO, SEQS, LEN, D)
    layer_out = jnp.stack([firsts.reshape(shape_out), seconds.reshape(shape_out)]).astype(jnp.bfloat16)
    input_grads = jnp.stack([gradients[0].reshape(shape_out), gradients[1].reshape(shape_out)]).astype(jnp.bfloat16)
    return (layer_out, input_grads, gradients[2], gradients[3], gradients[4], gradients[5], gradients[6], gradients[7], gradients[8])
```

```python
import jax
import jax.numpy as jnp
from jax import lax
from jax.sharding import PartitionSpec as P

D = 768
HEADS = 12
HEAD_DIM = 64
ROT = 16
FF = 3072
BF = jnp.bfloat16
F32 = jnp.float32


def pick(stack, index, axis=0):
    return lax.dynamic_index_in_dim(stack, index, axis, keepdims=False)


def swap_cores(block):
    return lax.ppermute(block, "section", [(0, 1), (1, 0)])


def along_ctx(block, step):
    count = lax.axis_size("ctx")
    return lax.ppermute(block, "ctx", [(i, i ^ step) for i in range(count)])


def along_square(block):
    count = lax.axis_size("fsdp")
    route = [(core * count + i, core * count + (i ^ (1 + core))) for core in (0, 1) for i in range(count)]
    return lax.ppermute(block, ("section", "fsdp"), route)


def across_halves(block, source_core, target_core):
    count = lax.axis_size("ctx")
    route = [
        (source_core * count + i, target_core * count + (i + count // 2) % count)
        for i in range(count)
    ]
    return lax.ppermute(block, ("section", "ctx"), route)


def half_columns(block, which):
    width = block.shape[-1] // 2
    return lax.dynamic_slice_in_dim(block, which * width, width, block.ndim - 1)


def gather_matrix(shard, core, place):
    rows, cols = shard.shape
    mine = along_square(shard)
    theirs = swap_cores(mine)
    halved = theirs.reshape(2, rows // 2, cols)
    diag_mine = along_square(pick(halved, core))
    diag_theirs = swap_cores(diag_mine)
    whole = jnp.zeros((8, rows // 2, cols), shard.dtype)

    def put(whole, piece, index):
        return lax.dynamic_update_slice_in_dim(
            whole, piece.reshape(-1, rows // 2, cols), index, 0
        )

    whole = put(whole, shard, 2 * place)
    whole = put(whole, mine, 2 * (place ^ (1 + core)))
    whole = put(whole, theirs, 2 * (place ^ (2 - core)))
    whole = put(whole, diag_mine, 2 * (place ^ 3) + core)
    whole = put(whole, diag_theirs, 2 * (place ^ 3) + 1 - core)
    return whole.reshape(4 * rows, cols)


def gather_vectors(packed, core, place):
    own = [packed, *[
        lax.ppermute(packed, "fsdp", [(i, i ^ k) for i in range(4)]) for k in (1, 2, 3)
    ]]
    mine = jnp.stack(own)[place ^ jnp.arange(4)]
    theirs = swap_cores(mine)
    first = jnp.where(core == 0, mine, theirs)
    second = jnp.where(core == 0, theirs, mine)
    return first, second


def sum_over_square(parts, core, place):
    own = pick(parts, place, 1)
    mine = pick(parts, place ^ (1 + core), 1)
    theirs = pick(parts, place ^ (2 - core), 1)
    diag = pick(parts, place ^ 3, 1)
    mine_sib = swap_cores(theirs)
    diag_sib = swap_cores(half_columns(diag, 1 - core))
    diag_sum = half_columns(diag, core).astype(F32) + diag_sib.astype(F32)
    extra = swap_cores(along_square(diag_sum.astype(BF)))
    near = half_columns(mine, core).astype(F32) + half_columns(mine_sib, core).astype(F32)
    far = (
        half_columns(mine, 1 - core).astype(F32)
        + half_columns(mine_sib, 1 - core).astype(F32)
        + extra.astype(F32)
    )
    landed = along_square(jnp.stack([near, far]).astype(BF))
    give = half_columns(own, 1 - core).astype(F32) + landed[1].astype(F32)
    got = swap_cores(give.astype(BF))
    return half_columns(own, core).astype(F32) + landed[0].astype(F32) + got.astype(F32)


def sum_over_ctx(total, ctx_idx):
    count = lax.axis_size("ctx")
    step = 1
    while step < count:
        bit = (ctx_idx // step) % 2
        pairs = total.reshape(total.shape[0] // 2, 2, *total.shape[1:])
        sent = pick(pairs, 1 - bit, 1).astype(BF)
        total = pick(pairs, bit, 1) + along_ctx(sent, step).astype(F32)
        step *= 2
    return total[0]


def angle_tables(places):
    half_dims = ROT // 2
    frequency = 10000.0 ** (-(jnp.arange(half_dims, dtype=F32) * 2.0) / ROT)
    phases = places.astype(F32)[:, None] * frequency[None, :]
    phases = jnp.concatenate([phases, phases], -1)
    return (jnp.cos(phases)[:, None, :], jnp.sin(phases)[:, None, :])


def rotary(head_rows, cosine, sine):
    half_dims = ROT // 2
    rot_part = head_rows[..., :ROT]
    swapped = jnp.concatenate([-rot_part[..., half_dims:], rot_part[..., :half_dims]], -1)
    return jnp.concatenate([rot_part * cosine + swapped * sine, head_rows[..., ROT:]], -1)


def rotate_rows(rows, cosine, sine):
    heads = rows.reshape(rows.shape[0], HEADS, HEAD_DIM)
    return rotary(heads, cosine, sine).reshape(rows.shape)


def dot_f32(left, right):
    return jnp.dot(left, right, preferred_element_type=F32)


def dot_t(left, right):
    return lax.dot_general(left, right, (((1,), (1,)), ((), ())), preferred_element_type=F32)


def dot_rows(left, right):
    out = lax.dot_general(left, right, (((0,), (0,)), ((), ())), preferred_element_type=F32)
    return out.astype(BF)


def heads_of(rows):
    return rows.reshape(rows.shape[0], HEADS, HEAD_DIM)


def attention(query, key, value, allowed):
    scores = (
        jnp.einsum("qhd,khd->hqk", heads_of(query), heads_of(key), preferred_element_type=F32)
        * 0.125
    )
    scores = jnp.where(allowed, scores, -1e30)
    row_max = jnp.max(scores, -1, keepdims=True)
    exp_scores = jnp.exp(scores - row_max)
    row_sum = jnp.sum(exp_scores, -1, keepdims=True)
    probs = (exp_scores / row_sum).astype(BF)
    mixed = jnp.einsum("hqk,khd->qhd", probs, heads_of(value), preferred_element_type=F32)
    return mixed.reshape(query.shape).astype(BF), row_max, row_sum


def attention_back(query, key, value, allowed, row_max, row_sum, mixed_grad):
    q, k, v, dm = heads_of(query), heads_of(key), heads_of(value), heads_of(mixed_grad)
    scores = jnp.einsum("qhd,khd->hqk", q, k, preferred_element_type=F32) * 0.125
    scores = jnp.where(allowed, scores, -1e30)
    probs = jnp.exp(scores - row_max) / row_sum
    prob_grad = jnp.einsum("qhd,khd->hqk", dm, v, preferred_element_type=F32)
    centre = jnp.sum(probs * prob_grad, -1, keepdims=True)
    score_grad = (probs * (prob_grad - centre)).astype(BF)
    query_grad = jnp.einsum("hqk,khd->qhd", score_grad, k, preferred_element_type=F32) * 0.125
    key_grad = jnp.einsum("hqk,qhd->khd", score_grad, q, preferred_element_type=F32) * 0.125
    value_grad = jnp.einsum("hqk,qhd->khd", probs.astype(BF), dm, preferred_element_type=F32)
    return (
        query_grad.reshape(query.shape),
        key_grad.reshape(key.shape),
        value_grad.reshape(value.shape),
    )


def gelu_exact(up_rows):
    return jax.nn.gelu(up_rows, approximate=False)


def per_device(
    inputs,
    cotangent,
    block_order,
    norm_gain,
    norm_bias,
    qkv_weight,
    biases,
    out_weight,
    up_weight,
    down_weight,
):
    rows_dev = inputs.shape[2]
    core = lax.axis_index("section")
    ctx_idx = lax.axis_index("ctx")
    place = lax.axis_index("fsdp")
    ranks = lax.axis_size("ctx")
    squares = lax.axis_size("fsdp")
    group = ranks // 2
    micro = ctx_idx // group

    def rank_of(core_idx, ctx_of):
        return (ctx_of + core_idx * group) % ranks

    def places_of(rank):
        block = rows_dev // 2
        within = jnp.arange(rows_dev, dtype=jnp.int32)
        first = block_order[rank]
        block_ids = jnp.where(within < block, first, 2 * ranks - 1 - first)
        return block_ids * block + within % block

    def take_rows(whole):
        here = pick(whole[:, 0], micro)
        there = across_halves(pick(whole[:, 0], 1 - micro), 1, 1)
        return jnp.where(core == 0, here, there)

    def deliver(rows, layer):
        moved = across_halves(rows, 1, layer)
        here = rows if layer == 0 else lax.ppermute(rows, "section", [(0, 1)])
        first = jnp.where(micro == 0, here, moved)
        second = jnp.where(micro == 0, moved, here)
        return jnp.stack([first, second])

    packed = jnp.concatenate([norm_gain[0].reshape(-1), norm_bias[0].reshape(-1), biases[0]])
    vectors = gather_vectors(packed, core, place)
    shards = (qkv_weight[0], out_weight[0], up_weight[0], down_weight[0])
    siblings = [swap_cores(shard) for shard in shards]
    weights = []
    for layer in (0, 1):
        mats = [
            gather_matrix(jnp.where(core == layer, shard, sibling), core, place)
            for shard, sibling in zip(shards, siblings)
        ]
        vec = vectors[layer]
        width = norm_gain.shape[2]
        gains = [vec[:, j * width : (j + 1) * width].reshape(D) for j in (0, 1)]
        shifts = [vec[:, (2 + j) * width : (3 + j) * width].reshape(D) for j in (0, 1)]
        bias = vec[:, 4 * width :].reshape(-1)
        weights.append((mats, gains, shifts, bias))

    own_places = places_of(rank_of(core, ctx_idx))
    key_places = jnp.concatenate(
        [places_of(rank_of(one, ctx_idx ^ j)) for one in (core, 1 - core) for j in range(group)]
    )
    cosine, sine = angle_tables(own_places)
    allowed = (own_places[:, None] >= key_places[None, :])[None]

    tok_low = take_rows(inputs)
    top_grad = take_rows(cotangent)
    kept = []
    layer_outs = []
    for layer in (0, 1):
        (qkv_mat, out_mat, up_mat, down_mat), gains, shifts, bias = weights[layer]
        tok_rows = tok_low.astype(F32)
        row_mean = jnp.mean(tok_rows, -1, keepdims=True)
        centred = tok_rows - row_mean
        inverse = lax.rsqrt(jnp.mean(centred * centred, -1, keepdims=True) + 1e-05)
        normed = centred * inverse
        attn_in = (normed * gains[0] + shifts[0]).astype(BF)
        mlp_in = (normed * gains[1] + shifts[1]).astype(BF)
        qkv_rows = dot_f32(attn_in, qkv_mat) + bias[: 3 * D]
        query = rotate_rows(qkv_rows[:, :D], cosine, sine).astype(BF)
        key_rows = rotate_rows(qkv_rows[:, D : 2 * D], cosine, sine).astype(BF)
        value_rows = qkv_rows[:, 2 * D :].astype(BF)
        pair = jnp.concatenate([key_rows, value_rows], -1)
        near = [pair, *[along_ctx(pair, j) for j in range(1, group)]]
        far = [swap_cores(one) for one in near]
        every = jnp.concatenate(near + far)
        key, value = every[:, :D], every[:, D:]
        up_rows = dot_f32(mlp_in, up_mat) + bias[4 * D : 4 * D + FF]
        gelu_rows = gelu_exact(up_rows).astype(BF)
        mlp_rows = dot_f32(gelu_rows, down_mat) + bias[4 * D + FF :]
        mixed, row_max, row_sum = attention(query, key, value, allowed)
        attn_rows = dot_f32(mixed, out_mat) + bias[3 * D : 4 * D]
        tok_low = (tok_rows + (attn_rows + mlp_rows)).astype(BF)
        kept.append(
            (normed, inverse, attn_in, mlp_in, query, key, value, row_max, row_sum, mixed, up_rows, gelu_rows)
        )
        layer_outs.append(deliver(tok_low, layer))

    grad_low = top_grad
    grad_outs = [None, None]
    reduced = [None, None]
    blocks = ranks * squares

    def fold(grad):
        split = grad.reshape(ranks, squares, -1, grad.shape[1])
        return [split[..., j : j + D] for j in range(0, grad.shape[1], D)]

    for layer in (1, 0):
        (qkv_mat, out_mat, up_mat, down_mat), gains, shifts, bias = weights[layer]
        (normed, inverse, attn_in, mlp_in, query, key, value, row_max, row_sum, mixed, up_rows, gelu_rows) = kept[layer]
        mixed_grad = dot_t(grad_low, out_mat).astype(BF)
        query_grad, key_grad, value_grad = attention_back(
            query, key, value, allowed, row_max, row_sum, mixed_grad
        )
        pair_grad = jnp.concatenate([key_grad, value_grad], -1)
        local = pair_grad[: group * rows_dev]
        remote = pair_grad[group * rows_dev :].astype(BF)
        local = local + swap_cores(remote).astype(F32)
        total = local[:rows_dev]
        for j in range(1, group):
            sent = local[j * rows_dev : (j + 1) * rows_dev].astype(BF)
            total = total + along_ctx(sent, j).astype(F32)

        down_term = dot_rows(gelu_rows, grad_low)
        gelu_grad = dot_t(grad_low, down_mat)
        up_grad = jax.vjp(gelu_exact, up_rows)[1](gelu_grad)[0].astype(BF)
        up_term = dot_rows(mlp_in, up_grad)
        mlp_back = dot_t(up_grad, up_mat)
        out_term = dot_rows(mixed, grad_low)

        wide = jnp.concatenate(fold(down_term) + fold(up_term) , 2)
        wide = sum_over_ctx(sum_over_square(wide, core, place), ctx_idx)

        qkv_grad = jnp.concatenate(
            [
                rotate_rows(query_grad, cosine, -sine),
                rotate_rows(total[:, :D], cosine, -sine),
                total[:, D:],
            ],
            -1,
        ).astype(BF)
        qkv_term = dot_rows(attn_in, qkv_grad)
        attn_back = dot_t(qkv_grad, qkv_mat)
        norm_grad = attn_back * gains[0] + mlp_back * gains[1]
        centre = jnp.mean(norm_grad, -1, keepdims=True)
        along = jnp.mean(norm_grad * normed, -1, keepdims=True)
        back_rows = grad_low.astype(F32) + (norm_grad - centre - normed * along) * inverse
        gain_terms = [jnp.sum(attn_back * normed, 0), jnp.sum(mlp_back * normed, 0)]
        shift_terms = [jnp.sum(attn_back, 0), jnp.sum(mlp_back, 0)]
        grad_total = jnp.sum(grad_low.astype(F32), 0)
        bias_term = jnp.concatenate(
            [
                jnp.sum(qkv_grad.astype(F32), 0),
                grad_total,
                jnp.sum(up_grad.astype(F32), 0),
                grad_total,
            ]
        )
        small = jnp.concatenate(
            [one.reshape(blocks, -1) for one in gain_terms + shift_terms + [bias_term]], 1
        )
        small_width = small.shape[1]
        small = jnp.pad(small, ((0, 0), (0, 16 * D - small_width)))
        small = small.reshape(ranks, squares, 16, D).astype(BF)
        thin = jnp.concatenate(fold(qkv_term) + fold(out_term) + [small], 2)
        thin = sum_over_ctx(sum_over_square(thin, core, place), ctx_idx)
        grad_low = back_rows.astype(BF)
        grad_outs[layer] = deliver(grad_low, layer)
        reduced[layer] = (wide, thin)

    def finish(first, second):
        mine = jnp.where(core == 0, first, second)
        got = swap_cores(jnp.where(core == 0, second, first))
        return jnp.where(
            core == 0, jnp.concatenate([mine, got], -1), jnp.concatenate([got, mine], -1)
        )

    wide, thin = (finish(a, b) for a, b in zip(reduced[0], reduced[1]))
    down_rows = FF // blocks
    narrow = D // blocks

    def unfold(rows, count):
        return jnp.concatenate([rows[j * narrow : (j + 1) * narrow] for j in range(count)], -1)

    down_out = wide[:down_rows]
    up_out = unfold(wide[down_rows:], 4)
    qkv_out = unfold(thin, 3)
    out_out = thin[3 * narrow : 4 * narrow]
    small = thin[4 * narrow :].reshape(-1)[:small_width]
    gain_out = small[: 2 * narrow].reshape(2, narrow)
    shift_out = small[2 * narrow : 4 * narrow].reshape(2, narrow)
    bias_out = small[4 * narrow :]
    layer_out = jnp.where(core == 0, layer_outs[0], layer_outs[1])
    input_grads = jnp.where(core == 0, grad_outs[0], grad_outs[1])
    return (
        layer_out[None, :, None],
        input_grads[None, :, None],
        gain_out[None],
        shift_out[None],
        qkv_out[None],
        bias_out[None],
        out_out[None],
        up_out[None],
        down_out[None],
    )


def solution(mesh):
    in_specs = (
        P(None, "fsdp", "ctx", None),
        P(None, "fsdp", "ctx", None),
        P(),
        P("section", None, "fsdp"),
        P("section", None, "fsdp"),
        P("section", "fsdp", None),
        P("section", "fsdp"),
        P("section", "fsdp", None),
        P("section", "fsdp", None),
        P("section", "fsdp", None),
    )
    out_specs = (
        P("section", None, "fsdp", "ctx", None),
        P("section", None, "fsdp", "ctx", None),
        P("section", None, ("ctx", "fsdp")),
        P("section", None, ("ctx", "fsdp")),
        P("section", ("ctx", "fsdp"), None),
        P("section", ("ctx", "fsdp")),
        P("section", ("ctx", "fsdp"), None),
        P("section", ("ctx", "fsdp"), None),
        P("section", ("ctx", "fsdp"), None),
    )
    return jax.shard_map(
        per_device, mesh=mesh, in_specs=in_specs, out_specs=out_specs, check_vma=False
    )
```

```python
import jax
import jax.numpy as jnp
from jax import lax
from jax.experimental import pallas as pl
from jax.experimental.pallas import tpu as pltpu
from jax.sharding import PartitionSpec as P

D = 768
HEADS = 12
HEAD_DIM = 64
ROT = 16
FF = 3072
BF = jnp.bfloat16
F32 = jnp.float32


def pick(stack, index, axis=0):
    return lax.dynamic_index_in_dim(stack, index, axis, keepdims=False)


def swap_cores(block):
    return lax.ppermute(block, "section", [(0, 1), (1, 0)])


def along_ctx(block, step):
    count = lax.axis_size("ctx")
    return lax.ppermute(block, "ctx", [(i, i ^ step) for i in range(count)])


def along_square(block):
    count = lax.axis_size("fsdp")
    route = [(core * count + i, core * count + (i ^ (1 + core))) for core in (0, 1) for i in range(count)]
    return lax.ppermute(block, ("section", "fsdp"), route)


def across_halves(block, source_core, target_core):
    count = lax.axis_size("ctx")
    route = [
        (source_core * count + i, target_core * count + (i + count // 2) % count)
        for i in range(count)
    ]
    return lax.ppermute(block, ("section", "ctx"), route)


def half_columns(block, which):
    width = block.shape[-1] // 2
    return lax.dynamic_slice_in_dim(block, which * width, width, block.ndim - 1)


def tied(value, *others):
    return lax.optimization_barrier((value, *others))[0]


def place_pieces(index_ref, *refs):
    pieces, whole, sems = refs[:-2], refs[-2], refs[-1]
    copies = []
    for j, piece in enumerate(pieces):
        target = whole.at[pl.ds(index_ref[j], piece.shape[0])]
        copies.append(pltpu.make_async_copy(piece, target, sems.at[j]))
    for copy in copies:
        copy.start()
    for copy in copies:
        copy.wait()


def assemble(pieces, indices):
    rows, cols = pieces[0].shape[1:]
    return pl.pallas_call(
        place_pieces,
        out_shape=jax.ShapeDtypeStruct((8, rows, cols), pieces[0].dtype),
        in_specs=[pl.BlockSpec(memory_space=pltpu.SMEM)]
        + [pl.BlockSpec(memory_space=pl.ANY)] * len(pieces),
        out_specs=pl.BlockSpec(memory_space=pltpu.VMEM),
        scratch_shapes=[pltpu.SemaphoreType.DMA((len(pieces),))],
        compiler_params=pltpu.CompilerParams(vmem_limit_bytes=16 * 2**20),
        cost_estimate=pl.CostEstimate(
            flops=0, bytes_accessed=2 * 8 * rows * cols * 2, transcendentals=0
        ),
    )(jnp.stack(indices).astype(jnp.int32), *pieces)


class SquareQueue:
    def __init__(self):
        self.landed = []

    def send(self, block):
        if len(self.landed) >= 2:
            block = tied(block, self.landed[-2])
        self.landed.append(along_square(block))
        return self.landed[-1]


def gather_weights(layers, core, place):
    queue = SquareQueue()
    waiting = []
    done = []

    def forward(entry):
        shard, mine = entry
        rows, cols = shard.shape
        theirs = swap_cores(mine)
        diag_mine = queue.send(pick(theirs.reshape(2, rows // 2, cols), core))
        diag_theirs = swap_cores(diag_mine)
        pieces = [
            one.reshape(-1, rows // 2, cols)
            for one in (shard, mine, theirs, diag_mine, diag_theirs)
        ]
        whole = assemble(
            pieces,
            [
                2 * place,
                2 * (place ^ (1 + core)),
                2 * (place ^ (2 - core)),
                2 * (place ^ 3) + core,
                2 * (place ^ 3) + 1 - core,
            ],
        )
        done.append(whole.reshape(4 * rows, cols))

    for shards in layers:
        for shard in shards:
            waiting.append((shard, queue.send(shard)))
            if len(waiting) == 2:
                forward(waiting.pop(0))
    forward(waiting.pop(0))
    count = len(layers[0])
    return [done[i * count : (i + 1) * count] for i in range(len(layers))]


def gather_vectors(packed, core, place):
    own = [packed, *[
        lax.ppermute(packed, "fsdp", [(i, i ^ k) for i in range(4)]) for k in (1, 2, 3)
    ]]
    mine = jnp.stack(own)[place ^ jnp.arange(4)]
    theirs = swap_cores(mine)
    first = jnp.where(core == 0, mine, theirs)
    second = jnp.where(core == 0, theirs, mine)
    return first, second


def reduce_stages(parts, core, place, ctx_idx):
    own = pick(parts, place, 1)
    mine = pick(parts, place ^ (1 + core), 1)
    theirs = pick(parts, place ^ (2 - core), 1)
    diag = pick(parts, place ^ 3, 1)
    mine_sib = swap_cores(theirs)
    diag_sib = swap_cores(half_columns(diag, 1 - core))
    diag_sum = half_columns(diag, core).astype(F32) + diag_sib.astype(F32)
    landed = along_square(diag_sum.astype(BF))
    yield landed
    extra = swap_cores(landed)
    near = half_columns(mine, core).astype(F32) + half_columns(mine_sib, core).astype(F32)
    far = (
        half_columns(mine, 1 - core).astype(F32)
        + half_columns(mine_sib, 1 - core).astype(F32)
        + extra.astype(F32)
    )
    landed = along_square(jnp.stack([near, far]).astype(BF))
    yield landed
    give = half_columns(own, 1 - core).astype(F32) + landed[1].astype(F32)
    got = swap_cores(give.astype(BF))
    total = half_columns(own, core).astype(F32) + landed[0].astype(F32) + got.astype(F32)
    count = lax.axis_size("ctx")
    step = 1
    while step < count:
        bit = (ctx_idx // step) % 2
        pairs = total.reshape(total.shape[0] // 2, 2, *total.shape[1:])
        landed = along_ctx(pick(pairs, 1 - bit, 1).astype(BF), step)
        yield landed
        total = pick(pairs, bit, 1) + landed.astype(F32)
        step *= 2
    return total[0]


class Reduction:
    def __init__(self, *args):
        self.stages = reduce_stages(*args)
        self.result = None

    def step(self):
        try:
            return next(self.stages)
        except StopIteration as stop:
            self.result = stop.value
            return None

    def finish(self):
        while self.step() is not None:
            pass
        return self.result


LANES = 2 * HEAD_DIM
VMEM_LIMIT = 40 * 2**20


def rotary_tables(places, direction):
    half_dims = ROT // 2
    lane = jnp.arange(LANES) % HEAD_DIM
    frequency = 10000.0 ** (-((lane % half_dims).astype(F32) * 2.0) / ROT)
    phases = places.astype(F32)[:, None] * frequency[None, :]
    cosine = jnp.where(lane < ROT, jnp.cos(phases), 1.0)
    sine = jnp.sin(phases) * direction
    return (
        cosine,
        jnp.where(lane < half_dims, -sine, 0.0),
        jnp.where((lane >= half_dims) & (lane < ROT), sine, 0.0),
    )


def rotated(rows, cosine, right, left):
    width = rows.shape[1]
    return (
        rows * cosine
        + pltpu.roll(rows, width - ROT // 2, 1) * right
        + pltpu.roll(rows, ROT // 2, 1) * left
    )


def dot_nt(left, right):
    return lax.dot_general(left, right, (((1,), (1,)), ((), ())), preferred_element_type=F32)


def dot_tn(left, right):
    return lax.dot_general(left, right, (((0,), (0,)), ((), ())), preferred_element_type=F32)


def kernel_params():
    return pltpu.CompilerParams(vmem_limit_bytes=VMEM_LIMIT)


def qkv_kernel(in_ref, mat_ref, bias_ref, cos_ref, right_ref, left_ref, query_ref, pair_ref):
    rows = jnp.dot(in_ref[...], mat_ref[...], preferred_element_type=F32) + bias_ref[...]
    rows = rotated(rows, cos_ref[0], right_ref[0], left_ref[0]).astype(BF)
    step = pl.program_id(0)

    @pl.when(step < 3)
    def _():
        query_ref[...] = rows

    @pl.when(step >= 3)
    def _():
        pair_ref[...] = rows


def qkv_rows_of(attn_in, qkv_mat, bias, tables):
    count = attn_in.shape[0]
    table = pl.BlockSpec((1, count, 256), lambda j: (j // 3, 0, 0))
    return pl.pallas_call(
        qkv_kernel,
        grid=(9,),
        in_specs=[
            pl.BlockSpec((count, D), lambda j: (0, 0)),
            pl.BlockSpec((D, 256), lambda j: (0, j)),
            pl.BlockSpec((1, 256), lambda j: (0, j)),
            table,
            table,
            table,
        ],
        out_specs=[
            pl.BlockSpec((count, 256), lambda j: (0, jnp.minimum(j, 2))),
            pl.BlockSpec((count, 256), lambda j: (0, jnp.maximum(j - 3, 0))),
        ],
        out_shape=[
            jax.ShapeDtypeStruct((count, D), BF),
            jax.ShapeDtypeStruct((count, 2 * D), BF),
        ],
        compiler_params=kernel_params(),
        cost_estimate=pl.CostEstimate(
            flops=6 * count * D * D, bytes_accessed=6 * D * D, transcendentals=0
        ),
    )(attn_in, qkv_mat, bias[None], *tables)


def head_picks():
    lane = lax.broadcasted_iota(jnp.int32, (1, LANES), 1)
    first = jnp.where(lane < HEAD_DIM, 1.0, 0.0)
    return first.astype(BF), (1.0 - first).astype(BF)


def upper_lower(upper, lower):
    row = lax.broadcasted_iota(jnp.int32, upper.shape, 0)
    return jnp.where(row < HEAD_DIM, upper, lower).T


def attention_kernel(pieces, query_ref, *refs):
    keys, values = refs[:pieces], refs[pieces : 2 * pieces]
    mask_ref, mixed_ref, level_ref = refs[2 * pieces :]
    count = query_ref.shape[0]
    outs = []
    for head, chosen in enumerate(head_picks()):
        query = query_ref[...] * chosen
        scores = [
            dot_nt(key[...], query) + mask_ref[pl.ds(n * count, count), :]
            for n, key in enumerate(keys)
        ]
        top = scores[0].max(0, keepdims=True)
        for one in scores[1:]:
            top = jnp.maximum(top, one.max(0, keepdims=True))
        grown = [jnp.exp(one - top) for one in scores]
        total = grown[0].sum(0, keepdims=True)
        for one in grown[1:]:
            total = total + one.sum(0, keepdims=True)
        share = 1.0 / total
        out = dot_tn(values[0][...], (grown[0] * share).astype(BF))
        for value, one in zip(values[1:], grown[1:]):
            out = out + dot_tn(value[...], (one * share).astype(BF))
        level_ref[0, pl.ds(head, 1), :] = top + jnp.log(total)
        outs.append(out)
    mixed_ref[...] = upper_lower(*outs).astype(BF)


def piece_specs(count, pieces):
    key = pl.BlockSpec((count, LANES), lambda j: (0, j))
    value = pl.BlockSpec((count, LANES), lambda j: (0, j + D // LANES))
    return [key] * pieces + [value] * pieces


def attention(query, pairs, mask):
    count, pieces = query.shape[0], len(pairs)
    rows = pl.BlockSpec((count, LANES), lambda j: (0, j))
    work = count * count * pieces
    return pl.pallas_call(
        lambda *refs: attention_kernel(pieces, *refs),
        grid=(D // LANES,),
        in_specs=[rows, *piece_specs(count, pieces)]
        + [pl.BlockSpec(mask.shape, lambda j: (0, 0))],
        out_specs=[rows, pl.BlockSpec((1, 2, count), lambda j: (j, 0, 0))],
        out_shape=[
            jax.ShapeDtypeStruct((count, D), BF),
            jax.ShapeDtypeStruct((D // LANES, 2, count), F32),
        ],
        compiler_params=kernel_params(),
        cost_estimate=pl.CostEstimate(
            flops=16 * work * D, bytes_accessed=4 * work + 8 * count * D, transcendentals=HEADS * work
        ),
    )(query, *pairs, *pairs, mask)


def attention_back_kernel(pieces, query_ref, grad_ref, level_ref, *refs):
    keys, values = refs[:pieces], refs[pieces : 2 * pieces]
    mask_ref, cos_ref, right_ref, left_ref, query_out, near_ref, far_ref = refs[2 * pieces :]
    count = query_ref.shape[0]
    group = pieces // 2
    key_sums, value_sums = [None] * pieces, [None] * pieces
    query_sums = []
    for head, chosen in enumerate(head_picks()):
        query = query_ref[...] * chosen
        grad = grad_ref[...] * chosen
        level = level_ref[0, pl.ds(head, 1), :]
        probs, prob_grads = [], []
        centre = None
        for n in range(pieces):
            scores = dot_nt(keys[n][...], query) + mask_ref[pl.ds(n * count, count), :]
            probs.append(jnp.exp(scores - level))
            prob_grads.append(dot_nt(values[n][...], grad))
            part = (probs[n] * prob_grads[n]).sum(0, keepdims=True)
            centre = part if centre is None else centre + part
        query_sum = None
        for n in range(pieces):
            score_grad = (probs[n] * (prob_grads[n] - centre)).astype(BF)
            key_part = jnp.dot(score_grad, query, preferred_element_type=F32)
            value_part = jnp.dot(probs[n].astype(BF), grad, preferred_element_type=F32)
            part = dot_tn(keys[n][...], score_grad)
            query_sum = part if query_sum is None else query_sum + part
            key_sums[n] = key_part if head == 0 else key_sums[n] + key_part
            value_sums[n] = value_part if head == 0 else value_sums[n] + value_part
        query_sums.append(query_sum)
    for n in range(pieces):
        target = near_ref if n < group else far_ref
        target[n % group, 0] = key_sums[n].astype(BF)
        target[n % group, 1] = value_sums[n].astype(BF)
    query_grad = upper_lower(*query_sums) * 0.125
    query_out[...] = rotated(query_grad, cos_ref[...], right_ref[...], left_ref[...]).astype(BF)


def attention_back(query, pairs, mask, level, mixed_grad, tables):
    count, pieces = query.shape[0], len(pairs)
    group = pieces // 2
    rows = pl.BlockSpec((count, LANES), lambda j: (0, j))
    still = pl.BlockSpec((count, LANES), lambda j: (0, 0))
    moving = pl.BlockSpec((group, 2, count, LANES), lambda j: (0, 0, 0, j))
    work = count * count * pieces
    return pl.pallas_call(
        lambda *refs: attention_back_kernel(pieces, *refs),
        grid=(D // LANES,),
        in_specs=[rows, rows, pl.BlockSpec((1, 2, count), lambda j: (j, 0, 0))]
        + piece_specs(count, pieces)
        + [pl.BlockSpec(mask.shape, lambda j: (0, 0)), still, still, still],
        out_specs=[rows, moving, moving],
        out_shape=[
            jax.ShapeDtypeStruct((count, D), BF),
            jax.ShapeDtypeStruct((group, 2, count, D), BF),
            jax.ShapeDtypeStruct((group, 2, count, D), BF),
        ],
        compiler_params=kernel_params(),
        cost_estimate=pl.CostEstimate(
            flops=40 * work * D, bytes_accessed=4 * work + 20 * count * D, transcendentals=HEADS * work
        ),
    )(query, mixed_grad, level, *pairs, *pairs, mask, *tables)


def join_kernel(query_ref, cos_ref, right_ref, left_ref, *refs):
    parts, (out_ref, sum_ref) = refs[:-2], refs[-2:]
    for j in range(D // LANES):
        lanes = pl.ds(j * LANES, LANES)
        key, value = (
            sum((part[which, :, lanes].astype(F32) for part in parts[1:]), parts[0][which, :, lanes].astype(F32))
            for which in (0, 1)
        )
        key = rotated(key, cos_ref[...], right_ref[...], left_ref[...])
        for which, rows in enumerate((query_ref[:, lanes], key, value)):
            rows = rows.astype(BF)
            here = pl.ds(which * D + j * LANES, LANES)
            out_ref[:, here] = rows
            sum_ref[:, here] = rows.astype(F32).sum(0, keepdims=True)


def join_grads(query_grad, tables, parts):
    count = query_grad.shape[0]
    return pl.pallas_call(
        join_kernel,
        out_shape=[
            jax.ShapeDtypeStruct((count, 3 * D), BF),
            jax.ShapeDtypeStruct((1, 3 * D), F32),
        ],
        compiler_params=kernel_params(),
        cost_estimate=pl.CostEstimate(
            flops=10 * count * D, bytes_accessed=(12 + 4 * len(parts)) * count * D, transcendentals=0
        ),
    )(query_grad, *tables, *parts)


def dot_f32(left, right):
    return jnp.dot(left, right, preferred_element_type=F32)


def dot_t(left, right):
    return lax.dot_general(left, right, (((1,), (1,)), ((), ())), preferred_element_type=F32)


def dot_rows(left, right):
    out = lax.dot_general(left, right, (((0,), (0,)), ((), ())), preferred_element_type=F32)
    return out.astype(BF)


def gelu_and_slope(up_rows):
    below = 0.5 + 0.5 * lax.erf(up_rows * 0.7071067811865476)
    density = 0.3989422804014327 * jnp.exp(-0.5 * up_rows * up_rows)
    return (up_rows * below).astype(BF), below + up_rows * density


def per_device(
    inputs,
    cotangent,
    block_order,
    norm_gain,
    norm_bias,
    qkv_weight,
    biases,
    out_weight,
    up_weight,
    down_weight,
):
    rows_dev = inputs.shape[2]
    core = lax.axis_index("section")
    ctx_idx = lax.axis_index("ctx")
    place = lax.axis_index("fsdp")
    ranks = lax.axis_size("ctx")
    squares = lax.axis_size("fsdp")
    group = ranks // 2
    micro = ctx_idx // group

    def rank_of(core_idx, ctx_of):
        return (ctx_of + core_idx * group) % ranks

    def places_of(rank):
        block = rows_dev // 2
        within = jnp.arange(rows_dev, dtype=jnp.int32)
        first = block_order[rank]
        block_ids = jnp.where(within < block, first, 2 * ranks - 1 - first)
        return block_ids * block + within % block

    def take_rows(whole):
        here = pick(whole[:, 0], micro)
        there = across_halves(pick(whole[:, 0], 1 - micro), 1, 1)
        return jnp.where(core == 0, here, there)

    def deliver(rows, layer):
        moved = across_halves(rows, 1, layer)
        here = rows if layer == 0 else lax.ppermute(rows, "section", [(0, 1)])
        first = jnp.where(micro == 0, here, moved)
        second = jnp.where(micro == 0, moved, here)
        return jnp.stack([first, second])

    packed = jnp.concatenate([norm_gain[0].reshape(-1), norm_bias[0].reshape(-1), biases[0]])
    vectors = gather_vectors(packed, core, place)
    shards = (qkv_weight[0], up_weight[0], down_weight[0], out_weight[0])
    siblings = [swap_cores(shard) for shard in shards]
    matrices = gather_weights(
        [
            [jnp.where(core == layer, *pair) for pair in zip(shards, siblings)]
            for layer in (0, 1)
        ],
        core,
        place,
    )
    weights = []
    for layer in (0, 1):
        vec = vectors[layer]
        width = norm_gain.shape[2]
        gains = [vec[:, j * width : (j + 1) * width].reshape(D) for j in (0, 1)]
        shifts = [vec[:, (2 + j) * width : (3 + j) * width].reshape(D) for j in (0, 1)]
        bias = vec[:, 4 * width :].reshape(-1)
        weights.append((matrices[layer], gains, shifts, bias))

    own_places = places_of(rank_of(core, ctx_idx))
    key_places = jnp.concatenate(
        [places_of(rank_of(one, ctx_idx ^ j)) for one in (core, 1 - core) for j in range(group)]
    )
    ahead = rotary_tables(own_places, 1.0)
    back = rotary_tables(own_places, -1.0)
    still = (jnp.ones_like(ahead[0]), jnp.zeros_like(ahead[0]), jnp.zeros_like(ahead[0]))
    tables = [
        jnp.stack([jnp.tile(one, (1, 2)) for one in (ahead[k] * 0.125, ahead[k], still[k])])
        for k in range(3)
    ]
    mask = jnp.where(own_places[None, :] >= key_places[:, None], 0.0, -1e30)

    tok_low = take_rows(inputs)
    top_grad = take_rows(cotangent)
    kept = []
    layer_outs = []
    for layer in (0, 1):
        (qkv_mat, up_mat, down_mat, out_mat), gains, shifts, bias = weights[layer]
        tok_rows = tok_low.astype(F32)
        row_mean = jnp.mean(tok_rows, -1, keepdims=True)
        centred = tok_rows - row_mean
        inverse = lax.rsqrt(jnp.mean(centred * centred, -1, keepdims=True) + 1e-05)
        normed = centred * inverse
        attn_in = (normed * gains[0] + shifts[0]).astype(BF)
        mlp_in = (normed * gains[1] + shifts[1]).astype(BF)
        query, pair = qkv_rows_of(attn_in, qkv_mat, bias[: 3 * D], tables)
        near = [pair, *[along_ctx(pair, j) for j in range(1, group)]]
        pairs = near + [swap_cores(one) for one in near]
        up_rows = dot_f32(mlp_in, up_mat) + bias[4 * D : 4 * D + FF]
        gelu_rows, slope = gelu_and_slope(up_rows)
        mlp_rows = dot_f32(gelu_rows, down_mat) + bias[4 * D + FF :]
        mixed, level = attention(query, pairs, mask)
        attn_rows = dot_f32(mixed, out_mat) + bias[3 * D : 4 * D]
        tok_low = (tok_rows + (attn_rows + mlp_rows)).astype(BF)
        kept.append(
            (normed, inverse, attn_in, mlp_in, query, pairs, level, mixed, slope, gelu_rows)
        )
        layer_outs.append(deliver(tok_low, layer))

    grad_low = top_grad
    grad_outs = [None, None]
    blocks = ranks * squares

    def fold(grad):
        split = grad.reshape(ranks, squares, -1, grad.shape[1])
        return [split[..., j : j + D] for j in range(0, grad.shape[1], D)]

    wide = [None, None]
    thin = [None, None]
    for layer in (1, 0):
        (qkv_mat, up_mat, down_mat, out_mat), gains, shifts, bias = weights[layer]
        (normed, inverse, attn_in, mlp_in, query, pairs, level, mixed, slope, gelu_rows) = kept[layer]
        down_term = dot_rows(gelu_rows, grad_low)
        up_grad = (dot_t(grad_low, down_mat) * slope).astype(BF)
        up_term = dot_rows(mlp_in, up_grad)
        parts = jnp.concatenate(fold(down_term) + fold(up_term), 2)
        wide[layer] = Reduction(parts, core, place, ctx_idx)
        first = wide[layer].step()
        mlp_back = dot_t(up_grad, up_mat)
        mixed_grad = dot_t(grad_low, out_mat).astype(BF)
        if layer == 0:
            mixed_grad = tied(mixed_grad, thin[1].step(), wide[1].step(), layer_outs[1])
        query_grad, near, far = attention_back(query, pairs, mask, level, mixed_grad, back)
        if layer == 1:
            far = tied(far, first, layer_outs[0])
        else:
            far = tied(far, first, thin[1].step(), grad_outs[1])
        far = swap_cores(far)
        parts = [near[0], far[0]]
        for j in range(1, group):
            sent = (near[j].astype(F32) + far[j].astype(F32)).astype(BF)
            parts.append(along_ctx(sent, j))
        qkv_grad, qkv_sums = join_grads(query_grad, back, parts)
        out_term = dot_rows(mixed, grad_low)

        qkv_term = dot_rows(attn_in, qkv_grad)
        attn_back = dot_t(qkv_grad, qkv_mat)
        attn_back = tied(attn_back, wide[layer].step())
        norm_grad = attn_back * gains[0] + mlp_back * gains[1]
        centre = jnp.mean(norm_grad, -1, keepdims=True)
        along = jnp.mean(norm_grad * normed, -1, keepdims=True)
        back_rows = grad_low.astype(F32) + (norm_grad - centre - normed * along) * inverse
        gain_terms = [jnp.sum(attn_back * normed, 0), jnp.sum(mlp_back * normed, 0)]
        shift_terms = [jnp.sum(attn_back, 0), jnp.sum(mlp_back, 0)]
        grad_total = jnp.sum(grad_low.astype(F32), 0)
        bias_term = jnp.concatenate(
            [
                qkv_sums[0],
                grad_total,
                jnp.sum(up_grad.astype(F32), 0),
                grad_total,
            ]
        )
        small = jnp.concatenate(
            [one.reshape(blocks, -1) for one in gain_terms + shift_terms + [bias_term]], 1
        )
        small_width = small.shape[1]
        small = jnp.pad(small, ((0, 0), (0, 16 * D - small_width)))
        small = small.reshape(ranks, squares, 16, D).astype(BF)
        parts = jnp.concatenate(fold(qkv_term) + fold(out_term) + [small], 2)
        thin[layer] = Reduction(parts, core, place, ctx_idx)
        grad_low = back_rows.astype(BF)
        grad_outs[layer] = deliver(grad_low, layer)

    def finish(first, second):
        mine = jnp.where(core == 0, first, second)
        got = swap_cores(jnp.where(core == 0, second, first))
        return jnp.where(
            core == 0, jnp.concatenate([mine, got], -1), jnp.concatenate([got, mine], -1)
        )

    wide, thin = (finish(pair[0].finish(), pair[1].finish()) for pair in (wide, thin))
    down_rows = FF // blocks
    narrow = D // blocks

    def unfold(rows, count):
        return jnp.concatenate([rows[j * narrow : (j + 1) * narrow] for j in range(count)], -1)

    down_out = wide[:down_rows]
    up_out = unfold(wide[down_rows:], 4)
    qkv_out = unfold(thin, 3)
    out_out = thin[3 * narrow : 4 * narrow]
    small = thin[4 * narrow :].reshape(-1)[:small_width]
    gain_out = small[: 2 * narrow].reshape(2, narrow)
    shift_out = small[2 * narrow : 4 * narrow].reshape(2, narrow)
    bias_out = small[4 * narrow :]
    layer_out = jnp.where(core == 0, layer_outs[0], layer_outs[1])
    input_grads = jnp.where(core == 0, grad_outs[0], grad_outs[1])
    return (
        layer_out[None, :, None],
        input_grads[None, :, None],
        gain_out[None],
        shift_out[None],
        qkv_out[None],
        bias_out[None],
        out_out[None],
        up_out[None],
        down_out[None],
    )


def solution(mesh):
    in_specs = (
        P(None, "fsdp", "ctx", None),
        P(None, "fsdp", "ctx", None),
        P(),
        P("section", None, "fsdp"),
        P("section", None, "fsdp"),
        P("section", "fsdp", None),
        P("section", "fsdp"),
        P("section", "fsdp", None),
        P("section", "fsdp", None),
        P("section", "fsdp", None),
    )
    out_specs = (
        P("section", None, "fsdp", "ctx", None),
        P("section", None, "fsdp", "ctx", None),
        P("section", None, ("ctx", "fsdp")),
        P("section", None, ("ctx", "fsdp")),
        P("section", ("ctx", "fsdp"), None),
        P("section", ("ctx", "fsdp")),
        P("section", ("ctx", "fsdp"), None),
        P("section", ("ctx", "fsdp"), None),
        P("section", ("ctx", "fsdp"), None),
    )
    return jax.shard_map(
        per_device, mesh=mesh, in_specs=in_specs, out_specs=out_specs, check_vma=False
    )
```

```python
import jax
import jax.numpy as jnp
from jax import lax
from jax.experimental import pallas as pl
from jax.experimental.pallas import tpu as pltpu
from jax.sharding import PartitionSpec as P

D = 768
HEADS = 12
HEAD_DIM = 64
ROT = 16
FF = 3072
BF = jnp.bfloat16
F32 = jnp.float32


def pick(stack, index, axis=0):
    return lax.dynamic_index_in_dim(stack, index, axis, keepdims=False)


def swap_cores(block):
    return lax.ppermute(block, "section", [(0, 1), (1, 0)])


def along_ctx(block, step):
    count = lax.axis_size("ctx")
    return lax.ppermute(block, "ctx", [(i, i ^ step) for i in range(count)])


def along_square(block):
    count = lax.axis_size("fsdp")
    route = [(core * count + i, core * count + (i ^ (1 + core))) for core in (0, 1) for i in range(count)]
    return lax.ppermute(block, ("section", "fsdp"), route)


def across_halves(block, source_core, target_core):
    count = lax.axis_size("ctx")
    route = [
        (source_core * count + i, target_core * count + (i + count // 2) % count)
        for i in range(count)
    ]
    return lax.ppermute(block, ("section", "ctx"), route)


def half_columns(block, which):
    width = block.shape[-1] // 2
    return lax.dynamic_slice_in_dim(block, which * width, width, block.ndim - 1)


def tied(value, *others):
    return lax.optimization_barrier((value, *others))[0]


def together(*values):
    return lax.optimization_barrier(values)


def place_pieces(first, cut, index_ref, *refs):
    pieces, whole, sems = refs[:-2], refs[-2], refs[-1]
    width = whole.shape[2]
    copies = []
    for j, piece in enumerate(pieces):
        halves = piece.shape[0]
        index = index_ref[j]
        for part in range(cut):
            target = (index // 2) * (2 * cut) + 2 * part + index % 2
            copies.append(
                pltpu.make_async_copy(
                    piece.at[:, :, pl.ds(first + part * width, width)],
                    whole.at[pl.ds(target, halves)],
                    sems.at[j * cut + part],
                )
            )
    for copy in copies:
        copy.start()
    for copy in copies:
        copy.wait()


def assemble(pieces, indices, first, cut, width):
    rows = pieces[0].shape[1]
    whole = pl.pallas_call(
        lambda *refs: place_pieces(first, cut, *refs),
        out_shape=jax.ShapeDtypeStruct((8 * cut, rows, width), pieces[0].dtype),
        in_specs=[pl.BlockSpec(memory_space=pltpu.SMEM)]
        + [pl.BlockSpec(memory_space=pl.ANY)] * len(pieces),
        out_specs=pl.BlockSpec(memory_space=pltpu.VMEM),
        scratch_shapes=[pltpu.SemaphoreType.DMA((len(pieces) * cut,))],
        compiler_params=pltpu.CompilerParams(vmem_limit_bytes=16 * 2**20),
        cost_estimate=pl.CostEstimate(flops=1, bytes_accessed=1, transcendentals=0),
    )(indices, *pieces)
    return whole.reshape(8 * cut * rows, width)


def gather_weights(blocks, core, place):
    firsts, pieces = [], []

    def second(block, mine):
        rows, cols = block.shape
        theirs = swap_cores(mine)
        diag_mine = along_square(pick(theirs.reshape(2, rows // 2, cols), core))
        diag_theirs = swap_cores(diag_mine)
        pieces.append(
            [
                one.reshape(-1, rows // 2, cols)
                for one in (block, mine, theirs, diag_mine, diag_theirs)
            ]
        )

    for block in blocks:
        if firsts:
            block = tied(block, firsts[-1][1])
        firsts.append((block, along_square(block)))
        if len(firsts) > 1:
            second(*firsts[-2])
    second(*firsts[-1])
    indices = jnp.stack(
        [
            2 * place,
            2 * (place ^ (1 + core)),
            2 * (place ^ (2 - core)),
            2 * (place ^ 3) + core,
            2 * (place ^ 3) + 1 - core,
        ]
    ).astype(jnp.int32)
    query, rest, early, late = pieces
    wide = 3 * D
    return [
        [
            assemble(query, indices, 0, 1, wide),
            assemble(rest, indices, 0, 1, FF),
            assemble(rest, indices, FF, 4, D),
            assemble(rest, indices, 2 * FF, 1, D),
        ],
        [
            assemble(early, indices, 0, 1, wide),
            assemble(early, indices, wide, 1, FF),
            assemble(late, indices, 0, 4, D),
            assemble(late, indices, FF, 1, D),
        ],
    ]


def gather_vectors(packed, core, place):
    own = [packed, *[
        lax.ppermute(packed, "fsdp", [(i, i ^ k) for i in range(4)]) for k in (1, 2, 3)
    ]]
    landed = own[1:]
    mine = jnp.stack(own)[place ^ jnp.arange(4)]
    theirs = swap_cores(mine)
    first = jnp.where(core == 0, mine, theirs)
    second = jnp.where(core == 0, theirs, mine)
    return (first, second), landed


def reduce_stages(parts, core, place, ctx_idx):
    own = pick(parts, place, 1)
    mine = pick(parts, place ^ (1 + core), 1)
    theirs = pick(parts, place ^ (2 - core), 1)
    diag = pick(parts, place ^ 3, 1)
    mine_sib = swap_cores(theirs)
    diag_sib = swap_cores(half_columns(diag, 1 - core))
    diag_sum = half_columns(diag, core).astype(F32) + diag_sib.astype(F32)
    landed = yield along_square(diag_sum.astype(BF))
    extra = swap_cores(landed)
    near = half_columns(mine, core).astype(F32) + half_columns(mine_sib, core).astype(F32)
    far = (
        half_columns(mine, 1 - core).astype(F32)
        + half_columns(mine_sib, 1 - core).astype(F32)
        + extra.astype(F32)
    )
    landed = yield along_square(jnp.stack([near, far]).astype(BF))
    give = half_columns(own, 1 - core).astype(F32) + landed[1].astype(F32)
    got = swap_cores(give.astype(BF))
    total = half_columns(own, core).astype(F32) + landed[0].astype(F32) + got.astype(F32)
    count = lax.axis_size("ctx")
    step = 1
    while step < count:
        bit = (ctx_idx // step) % 2
        pairs = total.reshape(total.shape[0] // 2, 2, *total.shape[1:])
        landed = yield along_ctx(pick(pairs, 1 - bit, 1).astype(BF), step)
        total = pick(pairs, bit, 1) + landed.astype(F32)
        step *= 2
    return total[0]


class Reduction:
    def __init__(self, *args):
        self.stages = reduce_stages(*args)
        self.landed = next(self.stages)
        self.result = None

    def step(self):
        try:
            self.landed = self.stages.send(self.landed)
        except StopIteration as stop:
            self.result = stop.value
            self.landed = None

    def finish(self):
        while self.landed is not None:
            self.step()
        return self.result


def settle(reductions, *others):
    running = [one for one in reductions if one.landed is not None]
    values = together(*[one.landed for one in running], *others)
    for one, landed in zip(running, values):
        one.landed = landed
    return values[len(running) :]


LANES = 2 * HEAD_DIM
VMEM_LIMIT = 40 * 2**20


def rotary_tables(places, direction):
    half_dims = ROT // 2
    lane = jnp.arange(LANES) % HEAD_DIM
    frequency = 10000.0 ** (-((lane % half_dims).astype(F32) * 2.0) / ROT)
    phases = places.astype(F32)[:, None] * frequency[None, :]
    cosine = jnp.where(lane < ROT, jnp.cos(phases), 1.0)
    sine = jnp.sin(phases) * direction
    return (
        cosine,
        jnp.where(lane < half_dims, -sine, 0.0),
        jnp.where((lane >= half_dims) & (lane < ROT), sine, 0.0),
    )


def rotated(rows, cosine, right, left):
    width = rows.shape[1]
    return (
        rows * cosine
        + pltpu.roll(rows, width - ROT // 2, 1) * right
        + pltpu.roll(rows, ROT // 2, 1) * left
    )


def dot_nt(left, right):
    return lax.dot_general(left, right, (((1,), (1,)), ((), ())), preferred_element_type=F32)


def dot_tn(left, right):
    return lax.dot_general(left, right, (((0,), (0,)), ((), ())), preferred_element_type=F32)


def kernel_params():
    return pltpu.CompilerParams(vmem_limit_bytes=VMEM_LIMIT)


def qkv_kernel(in_ref, mat_ref, bias_ref, cos_ref, right_ref, left_ref, query_ref, pair_ref):
    rows = jnp.dot(in_ref[...], mat_ref[...], preferred_element_type=F32) + bias_ref[...]
    rows = rotated(rows, cos_ref[0], right_ref[0], left_ref[0]).astype(BF)
    step = pl.program_id(0)

    @pl.when(step < 3)
    def _():
        query_ref[...] = rows

    @pl.when(step >= 3)
    def _():
        pair_ref[...] = rows


def qkv_rows_of(attn_in, qkv_mat, bias, tables):
    count = attn_in.shape[0]
    table = pl.BlockSpec((1, count, 256), lambda j: (j // 3, 0, 0))
    return pl.pallas_call(
        qkv_kernel,
        grid=(9,),
        in_specs=[
            pl.BlockSpec((count, D), lambda j: (0, 0)),
            pl.BlockSpec((D, 256), lambda j: (0, j)),
            pl.BlockSpec((1, 256), lambda j: (0, j)),
            table,
            table,
            table,
        ],
        out_specs=[
            pl.BlockSpec((count, 256), lambda j: (0, jnp.minimum(j, 2))),
            pl.BlockSpec((count, 256), lambda j: (0, jnp.maximum(j - 3, 0))),
        ],
        out_shape=[
            jax.ShapeDtypeStruct((count, D), BF),
            jax.ShapeDtypeStruct((count, 2 * D), BF),
        ],
        compiler_params=kernel_params(),
        cost_estimate=pl.CostEstimate(flops=1, bytes_accessed=1, transcendentals=0),
    )(attn_in, qkv_mat, bias[None], *tables)


def head_picks():
    lane = lax.broadcasted_iota(jnp.int32, (1, LANES), 1)
    first = jnp.where(lane < HEAD_DIM, 1.0, 0.0)
    return first.astype(BF), (1.0 - first).astype(BF)


def upper_lower(upper, lower):
    row = lax.broadcasted_iota(jnp.int32, upper.shape, 0)
    return jnp.where(row < HEAD_DIM, upper, lower).T


def attention_kernel(pieces, query_ref, *refs):
    keys, values = refs[:pieces], refs[pieces : 2 * pieces]
    mask_ref, mixed_ref, level_ref = refs[2 * pieces :]
    count = query_ref.shape[0]
    outs = []
    for head, chosen in enumerate(head_picks()):
        query = query_ref[...] * chosen
        scores = [
            dot_nt(key[...], query) + mask_ref[pl.ds(n * count, count), :]
            for n, key in enumerate(keys)
        ]
        top = scores[0].max(0, keepdims=True)
        for one in scores[1:]:
            top = jnp.maximum(top, one.max(0, keepdims=True))
        grown = [jnp.exp(one - top) for one in scores]
        total = grown[0].sum(0, keepdims=True)
        for one in grown[1:]:
            total = total + one.sum(0, keepdims=True)
        share = 1.0 / total
        out = dot_tn(values[0][...], (grown[0] * share).astype(BF))
        for value, one in zip(values[1:], grown[1:]):
            out = out + dot_tn(value[...], (one * share).astype(BF))
        level_ref[0, pl.ds(head, 1), :] = top + jnp.log(total)
        outs.append(out)
    mixed_ref[...] = upper_lower(*outs).astype(BF)


def piece_specs(count, pieces):
    key = pl.BlockSpec((count, LANES), lambda j: (0, j))
    value = pl.BlockSpec((count, LANES), lambda j: (0, j + D // LANES))
    return [key] * pieces + [value] * pieces


def attention(query, pairs, mask):
    count, pieces = query.shape[0], len(pairs)
    rows = pl.BlockSpec((count, LANES), lambda j: (0, j))
    work = count * count * pieces
    return pl.pallas_call(
        lambda *refs: attention_kernel(pieces, *refs),
        grid=(D // LANES,),
        in_specs=[rows, *piece_specs(count, pieces)]
        + [pl.BlockSpec(mask.shape, lambda j: (0, 0))],
        out_specs=[rows, pl.BlockSpec((1, 2, count), lambda j: (j, 0, 0))],
        out_shape=[
            jax.ShapeDtypeStruct((count, D), BF),
            jax.ShapeDtypeStruct((D // LANES, 2, count), F32),
        ],
        compiler_params=kernel_params(),
        cost_estimate=pl.CostEstimate(flops=1, bytes_accessed=1, transcendentals=0),
    )(query, *pairs, *pairs, mask)


def attention_back_kernel(pieces, query_ref, grad_ref, level_ref, *refs):
    keys, values = refs[:pieces], refs[pieces : 2 * pieces]
    mask_ref, cos_ref, right_ref, left_ref, query_out, near_ref, far_ref = refs[2 * pieces :]
    count = query_ref.shape[0]
    group = pieces // 2
    key_sums, value_sums = [None] * pieces, [None] * pieces
    query_sums = []
    for head, chosen in enumerate(head_picks()):
        query = query_ref[...] * chosen
        grad = grad_ref[...] * chosen
        level = level_ref[0, pl.ds(head, 1), :]
        probs, prob_grads = [], []
        centre = None
        for n in range(pieces):
            scores = dot_nt(keys[n][...], query) + mask_ref[pl.ds(n * count, count), :]
            probs.append(jnp.exp(scores - level))
            prob_grads.append(dot_nt(values[n][...], grad))
            part = (probs[n] * prob_grads[n]).sum(0, keepdims=True)
            centre = part if centre is None else centre + part
        query_sum = None
        for n in range(pieces):
            score_grad = (probs[n] * (prob_grads[n] - centre)).astype(BF)
            key_part = jnp.dot(score_grad, query, preferred_element_type=F32)
            value_part = jnp.dot(probs[n].astype(BF), grad, preferred_element_type=F32)
            part = dot_tn(keys[n][...], score_grad)
            query_sum = part if query_sum is None else query_sum + part
            key_sums[n] = key_part if head == 0 else key_sums[n] + key_part
            value_sums[n] = value_part if head == 0 else value_sums[n] + value_part
        query_sums.append(query_sum)
    for n in range(pieces):
        target = near_ref if n < group else far_ref
        target[n % group, 0] = key_sums[n].astype(BF)
        target[n % group, 1] = value_sums[n].astype(BF)
    query_grad = upper_lower(*query_sums) * 0.125
    query_out[...] = rotated(query_grad, cos_ref[...], right_ref[...], left_ref[...]).astype(BF)


def attention_back(query, pairs, mask, level, mixed_grad, tables):
    count, pieces = query.shape[0], len(pairs)
    group = pieces // 2
    rows = pl.BlockSpec((count, LANES), lambda j: (0, j))
    still = pl.BlockSpec((count, LANES), lambda j: (0, 0))
    moving = pl.BlockSpec((group, 2, count, LANES), lambda j: (0, 0, 0, j))
    work = count * count * pieces
    return pl.pallas_call(
        lambda *refs: attention_back_kernel(pieces, *refs),
        grid=(D // LANES,),
        in_specs=[rows, rows, pl.BlockSpec((1, 2, count), lambda j: (j, 0, 0))]
        + piece_specs(count, pieces)
        + [pl.BlockSpec(mask.shape, lambda j: (0, 0)), still, still, still],
        out_specs=[rows, moving, moving],
        out_shape=[
            jax.ShapeDtypeStruct((count, D), BF),
            jax.ShapeDtypeStruct((group, 2, count, D), BF),
            jax.ShapeDtypeStruct((group, 2, count, D), BF),
        ],
        compiler_params=kernel_params(),
        cost_estimate=pl.CostEstimate(flops=1, bytes_accessed=1, transcendentals=0),
    )(query, mixed_grad, level, *pairs, *pairs, mask, *tables)


def join_kernel(query_ref, cos_ref, right_ref, left_ref, *refs):
    parts, (out_ref, sum_ref) = refs[:-2], refs[-2:]
    for j in range(D // LANES):
        lanes = pl.ds(j * LANES, LANES)
        key, value = (
            sum((part[which, :, lanes].astype(F32) for part in parts[1:]), parts[0][which, :, lanes].astype(F32))
            for which in (0, 1)
        )
        key = rotated(key, cos_ref[...], right_ref[...], left_ref[...])
        for which, rows in enumerate((query_ref[:, lanes], key, value)):
            rows = rows.astype(BF)
            here = pl.ds(which * D + j * LANES, LANES)
            out_ref[:, here] = rows
            sum_ref[:, here] = rows.astype(F32).sum(0, keepdims=True)


def join_grads(query_grad, tables, parts):
    count = query_grad.shape[0]
    return pl.pallas_call(
        join_kernel,
        out_shape=[
            jax.ShapeDtypeStruct((count, 3 * D), BF),
            jax.ShapeDtypeStruct((1, 3 * D), F32),
        ],
        compiler_params=kernel_params(),
        cost_estimate=pl.CostEstimate(flops=1, bytes_accessed=1, transcendentals=0),
    )(query_grad, *tables, *parts)


def dot_f32(left, right):
    return jnp.dot(left, right, preferred_element_type=F32)


def dot_t(left, right):
    return lax.dot_general(left, right, (((1,), (1,)), ((), ())), preferred_element_type=F32)


def dot_rows(left, right):
    out = lax.dot_general(left, right, (((0,), (0,)), ((), ())), preferred_element_type=F32)
    return out.astype(BF)


def gelu_and_slope(up_rows):
    below = 0.5 + 0.5 * lax.erf(up_rows * 0.7071067811865476)
    density = 0.3989422804014327 * jnp.exp(-0.5 * up_rows * up_rows)
    return (up_rows * below).astype(BF), below + up_rows * density


def per_device(
    inputs,
    cotangent,
    block_order,
    norm_gain,
    norm_bias,
    qkv_weight,
    biases,
    out_weight,
    up_weight,
    down_weight,
):
    rows_dev = inputs.shape[2]
    core = lax.axis_index("section")
    ctx_idx = lax.axis_index("ctx")
    place = lax.axis_index("fsdp")
    ranks = lax.axis_size("ctx")
    squares = lax.axis_size("fsdp")
    group = ranks // 2
    micro = ctx_idx // group

    def rank_of(core_idx, ctx_of):
        return (ctx_of + core_idx * group) % ranks

    def places_of(rank):
        block = rows_dev // 2
        within = jnp.arange(rows_dev, dtype=jnp.int32)
        first = block_order[rank]
        block_ids = jnp.where(within < block, first, 2 * ranks - 1 - first)
        return block_ids * block + within % block

    def take_rows(whole):
        here = pick(whole[:, 0], micro)
        there = across_halves(pick(whole[:, 0], 1 - micro), 1, 1)
        return jnp.where(core == 0, here, there)

    def deliver(rows, layer):
        moved = across_halves(rows, 1, layer)
        here = rows if layer == 0 else lax.ppermute(rows, "section", [(0, 1)])
        first = jnp.where(micro == 0, here, moved)
        second = jnp.where(micro == 0, moved, here)
        return jnp.stack([first, second])

    packed = jnp.concatenate([norm_gain[0].reshape(-1), norm_bias[0].reshape(-1), biases[0]])
    vectors, vectors_landed = gather_vectors(packed, core, place)
    query_own = qkv_weight[0]
    query_sib = swap_cores(query_own)
    head = tied(jnp.where(core == 0, query_own, query_sib), *vectors_landed)
    slab = down_weight.shape[1] // 4
    rest_own = jnp.concatenate(
        [up_weight[0], *[down_weight[0, j * slab : (j + 1) * slab] for j in range(4)], out_weight[0]],
        -1,
    )
    rest_own = tied(rest_own, head)
    rest_sib = swap_cores(rest_own)
    rest_first = jnp.where(core == 0, rest_own, rest_sib)
    rest_next = jnp.where(core == 1, rest_own, rest_sib)
    query_next = jnp.where(core == 1, query_own, query_sib)
    blocks = [
        head,
        rest_first,
        jnp.concatenate([query_next, rest_next[:, :FF]], -1),
        rest_next[:, FF:],
    ]
    matrices = gather_weights(blocks, core, place)
    tok_low = take_rows(inputs)
    weights = []
    for layer in (0, 1):
        vec = vectors[layer]
        width = norm_gain.shape[2]
        gains = [vec[:, j * width : (j + 1) * width].reshape(D) for j in (0, 1)]
        shifts = [vec[:, (2 + j) * width : (3 + j) * width].reshape(D) for j in (0, 1)]
        bias = vec[:, 4 * width :].reshape(-1)
        biases_of = (bias[: 3 * D], bias[3 * D : 4 * D], bias[4 * D : 4 * D + FF], bias[4 * D + FF :])
        weights.append((matrices[layer], gains, shifts, biases_of))

    own_places = places_of(rank_of(core, ctx_idx))
    key_places = jnp.concatenate(
        [places_of(rank_of(one, ctx_idx ^ j)) for one in (core, 1 - core) for j in range(group)]
    )
    ahead = rotary_tables(own_places, 1.0)
    back = rotary_tables(own_places, -1.0)
    still = (jnp.ones_like(ahead[0]), jnp.zeros_like(ahead[0]), jnp.zeros_like(ahead[0]))
    tables = [
        jnp.stack([jnp.tile(one, (1, 2)) for one in (ahead[k] * 0.125, ahead[k], still[k])])
        for k in range(3)
    ]
    mask = jnp.where(own_places[None, :] >= key_places[:, None], 0.0, -1e30)
    weights[0][0][0] = tied(
        weights[0][0][0], weights[0][1:], weights[1][1:], ahead, back, tables, mask
    )

    top_grad = take_rows(cotangent)
    kept = []
    layer_outs = []
    for layer in (0, 1):
        (qkv_mat, up_mat, down_mat, out_mat), gains, shifts, bias = weights[layer]
        tok_rows = tok_low.astype(F32)
        row_mean = jnp.mean(tok_rows, -1, keepdims=True)
        centred = tok_rows - row_mean
        inverse = lax.rsqrt(jnp.mean(centred * centred, -1, keepdims=True) + 1e-05)
        normed = centred * inverse
        attn_in = (normed * gains[0] + shifts[0]).astype(BF)
        mlp_in = (normed * gains[1] + shifts[1]).astype(BF)
        query, pair = qkv_rows_of(attn_in, qkv_mat, bias[0], tables)
        near = [pair, *[along_ctx(pair, j) for j in range(1, group)]]
        pairs = near + [swap_cores(one) for one in near]
        up_rows = dot_f32(mlp_in, up_mat) + bias[2]
        gelu_rows, slope = gelu_and_slope(up_rows)
        mlp_rows = dot_f32(gelu_rows, down_mat) + bias[3]
        mixed, level = attention(query, pairs, mask)
        attn_rows = dot_f32(mixed, out_mat) + bias[1]
        tok_low = (tok_rows + (attn_rows + mlp_rows)).astype(BF)
        kept.append(
            (normed, inverse, attn_in, mlp_in, query, pairs, level, mixed, slope, gelu_rows)
        )
        layer_outs.append(tok_low)

    grad_low = top_grad
    blocks = ranks * squares

    def fold(grad):
        split = grad.reshape(ranks, squares, -1, grad.shape[1])
        return [split[..., j : j + D] for j in range(0, grad.shape[1], D)]

    def enter(layer, grad_low):
        (qkv_mat, up_mat, down_mat, out_mat), gains, shifts, bias = weights[layer]
        mlp_in, slope, gelu_rows = kept[layer][3], kept[layer][8], kept[layer][9]
        down_term = dot_rows(gelu_rows, grad_low)
        up_grad = (dot_t(grad_low, down_mat) * slope).astype(BF)
        up_term = dot_rows(mlp_in, up_grad)
        wide = Reduction(
            jnp.concatenate(fold(down_term) + fold(up_term), 2), core, place, ctx_idx
        )
        return wide, up_grad, dot_t(grad_low, out_mat).astype(BF)

    def attend_back(layer, mixed_grad):
        query, pairs, level = kept[layer][4:7]
        return attention_back(query, pairs, mask, level, mixed_grad, back)

    def exchange(near, far):
        far = swap_cores(far)
        sent = [
            along_ctx((near[j].astype(F32) + far[j].astype(F32)).astype(BF), j)
            for j in range(1, group)
        ]
        return near[0], far[0], *sent

    def mlp_part(layer, grad_low, up_grad):
        up_mat = weights[layer][0][1]
        return dot_t(up_grad, up_mat), dot_rows(kept[layer][7], grad_low)

    def leave(layer, grad_low, qkv_grad, qkv_sums, mlp_back, up_grad):
        (qkv_mat, up_mat, down_mat, out_mat), gains, shifts, bias = weights[layer]
        normed, inverse = kept[layer][:2]
        attn_back = dot_t(qkv_grad, qkv_mat)
        norm_grad = attn_back * gains[0] + mlp_back * gains[1]
        centre = jnp.mean(norm_grad, -1, keepdims=True)
        along = jnp.mean(norm_grad * normed, -1, keepdims=True)
        back_rows = grad_low.astype(F32) + (norm_grad - centre - normed * along) * inverse
        gain_terms = [jnp.sum(attn_back * normed, 0), jnp.sum(mlp_back * normed, 0)]
        shift_terms = [jnp.sum(attn_back, 0), jnp.sum(mlp_back, 0)]
        grad_total = jnp.sum(grad_low.astype(F32), 0)
        bias_term = jnp.concatenate(
            [qkv_sums[0], grad_total, jnp.sum(up_grad.astype(F32), 0), grad_total]
        )
        small = jnp.concatenate(
            [one.reshape(blocks, -1) for one in gain_terms + shift_terms + [bias_term]], 1
        )
        small = jnp.pad(small, ((0, 0), (0, 16 * D - small.shape[1])))
        return back_rows.astype(BF), small.reshape(ranks, squares, 16, D).astype(BF)

    def reduction_of(parts):
        return Reduction(jnp.concatenate(parts, 2), core, place, ctx_idx)

    wide_1, up_grad, mixed_grad = enter(1, grad_low)
    query_grad, near, far = attend_back(1, mixed_grad)
    query_grad, near, far = settle([wide_1], query_grad, near, far)
    parts = exchange(near, far)
    wide_1.step()
    mlp_back, out_term = mlp_part(1, grad_low, up_grad)
    query_grad, mlp_back, out_term, *parts = settle([wide_1], query_grad, mlp_back, out_term, *parts)
    qkv_grad, qkv_sums = join_grads(query_grad, back, parts)
    low_grad, small = leave(1, grad_low, qkv_grad, qkv_sums, mlp_back, up_grad)
    qkv_term = dot_rows(kept[1][2], qkv_grad)
    thin_1 = reduction_of(fold(qkv_term) + fold(out_term) + [small])
    wide_1.step()

    wide_0, up_grad, mixed_grad = enter(0, low_grad)
    late = [deliver(low_grad, 1), *[deliver(one, j) for j, one in enumerate(layer_outs)]]
    mixed_grad, up_grad, *late = settle([thin_1, wide_1], mixed_grad, up_grad, *late)
    thin_1.step()
    wide_1.step()
    query_grad, near, far = attend_back(0, mixed_grad)
    query_grad, near, far = settle([wide_0, thin_1, wide_1], query_grad, near, far)
    parts = exchange(near, far)
    wide_0.step()
    thin_1.step()
    mlp_back, out_term = mlp_part(0, low_grad, up_grad)
    query_term = dot_rows(kept[0][2], query_grad)
    middle = reduction_of(fold(query_term) + fold(out_term))
    query_grad, mlp_back, *parts = settle(
        [wide_0, thin_1, middle], query_grad, mlp_back, *parts
    )
    qkv_grad, qkv_sums = join_grads(query_grad, back, parts)
    wide_0.step()
    thin_1.step()
    middle.step()
    qkv_term = dot_rows(kept[0][2], qkv_grad[:, D:])
    last_grad, small = leave(0, low_grad, qkv_grad, qkv_sums, mlp_back, up_grad)
    thin_0 = reduction_of(fold(qkv_term) + [small])
    (first_grads,) = settle([thin_0, wide_0, thin_1, middle], deliver(last_grad, 0))
    for one in (thin_0, wide_0, middle):
        one.step()
    settle([thin_0, wide_0, middle])
    grad_outs = [first_grads, late[0]]
    layer_outs = late[1:]
    small_width = (4 * D + biases.shape[1] * squares) // blocks

    def finish(first, second):
        mine = jnp.where(core == 0, first, second)
        got = swap_cores(jnp.where(core == 0, second, first))
        return jnp.where(
            core == 0, jnp.concatenate([mine, got], -1), jnp.concatenate([got, mine], -1)
        )

    narrow = D // blocks
    middle, low_thin = middle.finish(), thin_0.finish()
    low_thin = jnp.concatenate(
        [middle[:narrow], low_thin[: 2 * narrow], middle[narrow:], low_thin[2 * narrow :]]
    )
    wide = finish(wide_0.finish(), wide_1.finish())
    thin = finish(low_thin, thin_1.finish())
    down_rows = FF // blocks

    def unfold(rows, count):
        return jnp.concatenate([rows[j * narrow : (j + 1) * narrow] for j in range(count)], -1)

    down_out = wide[:down_rows]
    up_out = unfold(wide[down_rows:], 4)
    qkv_out = unfold(thin, 3)
    out_out = thin[3 * narrow : 4 * narrow]
    small = thin[4 * narrow :].reshape(-1)[:small_width]
    gain_out = small[: 2 * narrow].reshape(2, narrow)
    shift_out = small[2 * narrow : 4 * narrow].reshape(2, narrow)
    bias_out = small[4 * narrow :]
    layer_out = jnp.where(core == 0, layer_outs[0], layer_outs[1])
    input_grads = jnp.where(core == 0, grad_outs[0], grad_outs[1])
    return (
        layer_out[None, :, None],
        input_grads[None, :, None],
        gain_out[None],
        shift_out[None],
        qkv_out[None],
        bias_out[None],
        out_out[None],
        up_out[None],
        down_out[None],
    )


def solution(mesh):
    in_specs = (
        P(None, "fsdp", "ctx", None),
        P(None, "fsdp", "ctx", None),
        P(),
        P("section", None, "fsdp"),
        P("section", None, "fsdp"),
        P("section", "fsdp", None),
        P("section", "fsdp"),
        P("section", "fsdp", None),
        P("section", "fsdp", None),
        P("section", "fsdp", None),
    )
    out_specs = (
        P("section", None, "fsdp", "ctx", None),
        P("section", None, "fsdp", "ctx", None),
        P("section", None, ("ctx", "fsdp")),
        P("section", None, ("ctx", "fsdp")),
        P("section", ("ctx", "fsdp"), None),
        P("section", ("ctx", "fsdp")),
        P("section", ("ctx", "fsdp"), None),
        P("section", ("ctx", "fsdp"), None),
        P("section", ("ctx", "fsdp"), None),
    )
    return jax.shard_map(
        per_device, mesh=mesh, in_specs=in_specs, out_specs=out_specs, check_vma=False
    )
```

```python
import jax
import jax.numpy as jnp
from jax import lax
from jax.experimental import pallas as pl
from jax.experimental.pallas import tpu as pltpu
from jax.sharding import PartitionSpec as P

D = 768
HEADS = 12
HEAD_DIM = 64
ROT = 16
FF = 3072
BF = jnp.bfloat16
F32 = jnp.float32


def pick(stack, index, axis=0):
    return lax.dynamic_index_in_dim(stack, index, axis, keepdims=False)


def swap_cores(block):
    return lax.ppermute(block, "section", [(0, 1), (1, 0)])


def along_ctx(block, step):
    count = lax.axis_size("ctx")
    return lax.ppermute(block, "ctx", [(i, i ^ step) for i in range(count)])


def along_square(block):
    count = lax.axis_size("fsdp")
    route = [(core * count + i, core * count + (i ^ (1 + core))) for core in (0, 1) for i in range(count)]
    return lax.ppermute(block, ("section", "fsdp"), route)


def across_halves(block, source_core, target_core):
    count = lax.axis_size("ctx")
    route = [
        (source_core * count + i, target_core * count + (i + count // 2) % count)
        for i in range(count)
    ]
    return lax.ppermute(block, ("section", "ctx"), route)


def half_columns(block, which):
    width = block.shape[-1] // 2
    return lax.dynamic_slice_in_dim(block, which * width, width, block.ndim - 1)


def tied(value, *others):
    return lax.optimization_barrier((value, *others))[0]


def together(*values):
    return lax.optimization_barrier(values)


def place_pieces(first, cut, index_ref, *refs):
    pieces, whole, sems = refs[:-2], refs[-2], refs[-1]
    width = whole.shape[2]
    copies = []
    for j, piece in enumerate(pieces):
        halves = piece.shape[0]
        index = index_ref[j]
        for part in range(cut):
            target = (index // 2) * (2 * cut) + 2 * part + index % 2
            copies.append(
                pltpu.make_async_copy(
                    piece.at[:, :, pl.ds(first + part * width, width)],
                    whole.at[pl.ds(target, halves)],
                    sems.at[j * cut + part],
                )
            )
    for copy in copies:
        copy.start()
    for copy in copies:
        copy.wait()


def assemble(pieces, indices, first, cut, width):
    rows = pieces[0].shape[1]
    whole = pl.pallas_call(
        lambda *refs: place_pieces(first, cut, *refs),
        out_shape=jax.ShapeDtypeStruct((8 * cut, rows, width), pieces[0].dtype),
        in_specs=[pl.BlockSpec(memory_space=pltpu.SMEM)]
        + [pl.BlockSpec(memory_space=pl.ANY)] * len(pieces),
        out_specs=pl.BlockSpec(memory_space=pltpu.VMEM),
        scratch_shapes=[pltpu.SemaphoreType.DMA((len(pieces) * cut,))],
        compiler_params=pltpu.CompilerParams(vmem_limit_bytes=16 * 2**20),
        cost_estimate=pl.CostEstimate(flops=0, bytes_accessed=4 * 8 * cut * rows * width, transcendentals=0),
    )(indices, *pieces)
    return whole.reshape(8 * cut * rows, width)


def gather_weights(blocks, core, place):
    firsts, pieces = [], []

    def second(block, mine):
        rows, cols = block.shape
        theirs = swap_cores(mine)
        diag_mine = along_square(pick(theirs.reshape(2, rows // 2, cols), core))
        diag_theirs = swap_cores(diag_mine)
        pieces.append(
            [
                one.reshape(-1, rows // 2, cols)
                for one in (block, mine, theirs, diag_mine, diag_theirs)
            ]
        )

    for block in blocks:
        if firsts:
            block = tied(block, firsts[-1][1])
        firsts.append((block, along_square(block)))
        if len(firsts) > 1:
            second(*firsts[-2])
    second(*firsts[-1])
    indices = jnp.stack(
        [
            2 * place,
            2 * (place ^ (1 + core)),
            2 * (place ^ (2 - core)),
            2 * (place ^ 3) + core,
            2 * (place ^ 3) + 1 - core,
        ]
    ).astype(jnp.int32)
    query, rest, early, late = pieces
    wide = 3 * D
    return [
        [
            assemble(query, indices, 0, 1, wide),
            assemble(rest, indices, 0, 1, FF),
            assemble(rest, indices, FF, 4, D),
            assemble(rest, indices, 2 * FF, 1, D),
        ],
        [
            assemble(early, indices, 0, 1, wide),
            assemble(early, indices, wide, 1, FF),
            assemble(late, indices, 0, 4, D),
            assemble(late, indices, FF, 1, D),
        ],
    ]


def gather_vectors(packed, core, place):
    own = [packed, *[
        lax.ppermute(packed, "fsdp", [(i, i ^ k) for i in range(4)]) for k in (1, 2, 3)
    ]]
    landed = own[1:]
    mine = jnp.stack(own)[place ^ jnp.arange(4)]
    theirs = swap_cores(mine)
    first = jnp.where(core == 0, mine, theirs)
    second = jnp.where(core == 0, theirs, mine)
    return (first, second), landed


def reduce_stages(parts, core, place, ctx_idx):
    own = pick(parts, place, 1)
    mine = pick(parts, place ^ (1 + core), 1)
    theirs = pick(parts, place ^ (2 - core), 1)
    diag = pick(parts, place ^ 3, 1)
    mine_sib = swap_cores(theirs)
    diag_sib = swap_cores(half_columns(diag, 1 - core))
    diag_sum = half_columns(diag, core).astype(F32) + diag_sib.astype(F32)
    landed = yield along_square(diag_sum.astype(BF))
    extra = swap_cores(landed)
    near = half_columns(mine, core).astype(F32) + half_columns(mine_sib, core).astype(F32)
    far = (
        half_columns(mine, 1 - core).astype(F32)
        + half_columns(mine_sib, 1 - core).astype(F32)
        + extra.astype(F32)
    )
    landed = yield along_square(jnp.stack([near, far]).astype(BF))
    give = half_columns(own, 1 - core).astype(F32) + landed[1].astype(F32)
    got = swap_cores(give.astype(BF))
    total = half_columns(own, core).astype(F32) + landed[0].astype(F32) + got.astype(F32)
    count = lax.axis_size("ctx")
    step = 1
    while step < count:
        bit = (ctx_idx // step) % 2
        pairs = total.reshape(total.shape[0] // 2, 2, *total.shape[1:])
        landed = yield along_ctx(pick(pairs, 1 - bit, 1).astype(BF), step)
        total = pick(pairs, bit, 1) + landed.astype(F32)
        step *= 2
    return total[0]


class Reduction:
    def __init__(self, *args):
        self.stages = reduce_stages(*args)
        self.landed = next(self.stages)
        self.result = None

    def step(self):
        try:
            self.landed = self.stages.send(self.landed)
        except StopIteration as stop:
            self.result = stop.value
            self.landed = None

    def finish(self):
        while self.landed is not None:
            self.step()
        return self.result


def settle(reductions, *others):
    running = [one for one in reductions if one.landed is not None]
    values = together(*[one.landed for one in running], *others)
    for one, landed in zip(running, values):
        one.landed = landed
    return values[len(running) :]


LANES = 2 * HEAD_DIM
VMEM_LIMIT = 40 * 2**20


def rotary_tables(places, direction, width):
    half_dims = ROT // 2
    lane = jnp.arange(width) % HEAD_DIM
    frequency = 10000.0 ** (-((lane % half_dims).astype(F32) * 2.0) / ROT)
    phases = places.astype(F32)[:, None] * frequency[None, :]
    cosine = jnp.where(lane < ROT, jnp.cos(phases), 1.0)
    sine = jnp.sin(phases) * direction
    return (
        cosine,
        jnp.where(lane < half_dims, -sine, 0.0),
        jnp.where((lane >= half_dims) & (lane < ROT), sine, 0.0),
    )


def rotated(rows, cosine, right, left):
    width = rows.shape[1]
    return (
        rows * cosine
        + pltpu.roll(rows, width - ROT // 2, 1) * right
        + pltpu.roll(rows, ROT // 2, 1) * left
    )


def dot_nt(left, right):
    return lax.dot_general(left, right, (((1,), (1,)), ((), ())), preferred_element_type=F32)


def dot_tn(left, right):
    return lax.dot_general(left, right, (((0,), (0,)), ((), ())), preferred_element_type=F32)


def kernel_params():
    return pltpu.CompilerParams(vmem_limit_bytes=VMEM_LIMIT)


def qkv_kernel(in_ref, mat_ref, bias_ref, cos_ref, right_ref, left_ref, query_ref, pair_ref):
    rows = jnp.dot(in_ref[...], mat_ref[...], preferred_element_type=F32) + bias_ref[...]
    rows = rotated(rows, cos_ref[0], right_ref[0], left_ref[0]).astype(BF)
    step = pl.program_id(0)

    @pl.when(step < 3)
    def _():
        query_ref[...] = rows

    @pl.when(step >= 3)
    def _():
        pair_ref[...] = rows


def qkv_rows_of(attn_in, qkv_mat, bias, tables):
    count = attn_in.shape[0]
    table = pl.BlockSpec((1, count, 256), lambda j: (j // 3, 0, 0))
    return pl.pallas_call(
        qkv_kernel,
        grid=(9,),
        in_specs=[
            pl.BlockSpec((count, D), lambda j: (0, 0)),
            pl.BlockSpec((D, 256), lambda j: (0, j)),
            pl.BlockSpec((1, 256), lambda j: (0, j)),
            table,
            table,
            table,
        ],
        out_specs=[
            pl.BlockSpec((count, 256), lambda j: (0, jnp.minimum(j, 2))),
            pl.BlockSpec((count, 256), lambda j: (0, jnp.maximum(j - 3, 0))),
        ],
        out_shape=[
            jax.ShapeDtypeStruct((count, D), BF),
            jax.ShapeDtypeStruct((count, 2 * D), BF),
        ],
        compiler_params=kernel_params(),
        cost_estimate=pl.CostEstimate(flops=6 * count * D * D, bytes_accessed=6 * D * D, transcendentals=0),
    )(attn_in, qkv_mat, bias[None], *tables)


def head_picks():
    lane = lax.broadcasted_iota(jnp.int32, (1, LANES), 1)
    first = jnp.where(lane < HEAD_DIM, 1.0, 0.0)
    return first.astype(BF), (1.0 - first).astype(BF)


def upper_lower(upper, lower):
    row = lax.broadcasted_iota(jnp.int32, upper.shape, 0)
    return jnp.where(row < HEAD_DIM, upper, lower).T


def attention_kernel(pieces, query_ref, *refs):
    keys, values = refs[:pieces], refs[pieces : 2 * pieces]
    mask_ref, mixed_ref, level_ref = refs[2 * pieces :]
    count = query_ref.shape[0]
    outs = []
    for head, chosen in enumerate(head_picks()):
        query = query_ref[...] * chosen
        scores = [
            dot_nt(key[...], query) + mask_ref[pl.ds(n * count, count), :]
            for n, key in enumerate(keys)
        ]
        top = scores[0].max(0, keepdims=True)
        for one in scores[1:]:
            top = jnp.maximum(top, one.max(0, keepdims=True))
        grown = [jnp.exp(one - top) for one in scores]
        total = grown[0].sum(0, keepdims=True)
        for one in grown[1:]:
            total = total + one.sum(0, keepdims=True)
        share = 1.0 / total
        out = dot_tn(values[0][...], (grown[0] * share).astype(BF))
        for value, one in zip(values[1:], grown[1:]):
            out = out + dot_tn(value[...], (one * share).astype(BF))
        level_ref[0, pl.ds(head, 1), :] = top + jnp.log(total)
        outs.append(out)
    mixed_ref[...] = upper_lower(*outs).astype(BF)


def piece_specs(count, pieces):
    key = pl.BlockSpec((count, LANES), lambda j: (0, j))
    value = pl.BlockSpec((count, LANES), lambda j: (0, j + D // LANES))
    return [key] * pieces + [value] * pieces


def attention(query, pairs, mask):
    count, pieces = query.shape[0], len(pairs)
    rows = pl.BlockSpec((count, LANES), lambda j: (0, j))
    work = count * count * pieces
    return pl.pallas_call(
        lambda *refs: attention_kernel(pieces, *refs),
        grid=(D // LANES,),
        in_specs=[rows, *piece_specs(count, pieces)]
        + [pl.BlockSpec(mask.shape, lambda j: (0, 0))],
        out_specs=[rows, pl.BlockSpec((1, 2, count), lambda j: (j, 0, 0))],
        out_shape=[
            jax.ShapeDtypeStruct((count, D), BF),
            jax.ShapeDtypeStruct((D // LANES, 2, count), F32),
        ],
        compiler_params=kernel_params(),
        cost_estimate=pl.CostEstimate(flops=16 * count * count * len(pairs) * D, bytes_accessed=8 * count * D, transcendentals=0),
    )(query, *pairs, *pairs, mask)


def attention_back_kernel(chosen_rows, last, query_ref, grad_ref, mixed_ref, level_ref, *refs):
    pieces = len(chosen_rows)
    keys, values = refs[:pieces], refs[pieces : 2 * pieces]
    mask_ref, *tables, before_ref, query_out, near_ref, far_ref = refs[2 * pieces :]
    count = query_ref.shape[0]
    group = pieces // 2
    key_sums, value_sums = [None] * pieces, [None] * pieces
    query_sums = []
    products = (grad_ref[...].astype(F32) * mixed_ref[...].astype(F32)).T
    centres = [
        products[half : half + HEAD_DIM].sum(0, keepdims=True) for half in (0, HEAD_DIM)
    ]
    for head, chosen in enumerate(head_picks()):
        query = query_ref[...] * chosen
        grad = grad_ref[...] * chosen
        level = level_ref[0, pl.ds(head, 1), :]
        centre = centres[head]
        query_sum = None
        for n, place in enumerate(chosen_rows):
            scores = dot_nt(keys[n][...], query) + mask_ref[pl.ds(place * count, count), :]
            probs = jnp.exp(scores - level)
            score_grad = (probs * (dot_nt(values[n][...], grad) - centre)).astype(BF)
            key_part = jnp.dot(score_grad, query, preferred_element_type=F32)
            value_part = jnp.dot(probs.astype(BF), grad, preferred_element_type=F32)
            part = dot_tn(keys[n][...], score_grad)
            query_sum = part if query_sum is None else query_sum + part
            key_sums[n] = key_part if head == 0 else key_sums[n] + key_part
            value_sums[n] = value_part if head == 0 else value_sums[n] + value_part
        query_sums.append(query_sum)
    for n in range(pieces):
        target = near_ref if n < group else far_ref
        target[n % group, 0] = key_sums[n].astype(BF)
        target[n % group, 1] = value_sums[n].astype(BF)
    query_grad = upper_lower(*query_sums)
    if last:
        query_grad = (query_grad + before_ref[...]) * 0.125
        query_grad = rotated(query_grad, *[table[...] for table in tables])
    query_out[...] = query_grad.astype(query_out.dtype)


def attention_back(query, pairs, chosen_rows, mask, level, mixed, mixed_grad, tables, before):
    count, pieces = query.shape[0], len(chosen_rows)
    group = pieces // 2
    last = before is not None
    pairs = [pairs[n] for n in chosen_rows]
    rows = pl.BlockSpec((count, LANES), lambda j: (0, j))
    still = pl.BlockSpec((count, LANES), lambda j: (0, 0))
    moving = pl.BlockSpec((group, 2, count, LANES), lambda j: (0, 0, 0, j))
    return pl.pallas_call(
        lambda *refs: attention_back_kernel(chosen_rows, last, *refs),
        grid=(D // LANES,),
        in_specs=[rows, rows, rows, pl.BlockSpec((1, 2, count), lambda j: (j, 0, 0))]
        + piece_specs(count, pieces)
        + [pl.BlockSpec(mask.shape, lambda j: (0, 0)), still, still, still, rows if last else still],
        out_specs=[rows, moving, moving],
        out_shape=[
            jax.ShapeDtypeStruct((count, D), BF if last else F32),
            jax.ShapeDtypeStruct((group, 2, count, D), BF),
            jax.ShapeDtypeStruct((group, 2, count, D), BF),
        ],
        compiler_params=kernel_params(),
        cost_estimate=pl.CostEstimate(flops=1, bytes_accessed=1, transcendentals=0),
    )(
        query,
        mixed_grad,
        mixed,
        level,
        *pairs,
        *pairs,
        mask,
        *tables,
        before if last else tables[0],
    )


def join_kernel(query_ref, cos_ref, right_ref, left_ref, *refs):
    parts, (out_ref, sum_ref) = refs[:-2], refs[-2:]
    for j in range(D // LANES):
        lanes = pl.ds(j * LANES, LANES)
        key, value = (
            sum((part[which, :, lanes].astype(F32) for part in parts[1:]), parts[0][which, :, lanes].astype(F32))
            for which in (0, 1)
        )
        key = rotated(key, cos_ref[...], right_ref[...], left_ref[...])
        for which, rows in enumerate((query_ref[:, lanes], key, value)):
            rows = rows.astype(BF)
            here = pl.ds(which * D + j * LANES, LANES)
            out_ref[:, here] = rows
            sum_ref[:, here] = rows.astype(F32).sum(0, keepdims=True)


def join_grads(query_grad, tables, parts):
    count = query_grad.shape[0]
    return pl.pallas_call(
        join_kernel,
        out_shape=[
            jax.ShapeDtypeStruct((count, 3 * D), BF),
            jax.ShapeDtypeStruct((1, 3 * D), F32),
        ],
        compiler_params=kernel_params(),
        cost_estimate=pl.CostEstimate(flops=1, bytes_accessed=16 * count * D, transcendentals=0),
    )(query_grad, *tables, *parts)


def dot_f32(left, right):
    return jnp.dot(left, right, preferred_element_type=F32)


def dot_t(left, right):
    return lax.dot_general(left, right, (((1,), (1,)), ((), ())), preferred_element_type=F32)


def dot_rows(left, right):
    out = lax.dot_general(left, right, (((0,), (0,)), ((), ())), preferred_element_type=F32)
    return out.astype(BF)


def gelu_and_slope(up_rows):
    below = 0.5 + 0.5 * lax.erf(up_rows * 0.7071067811865476)
    density = 0.3989422804014327 * jnp.exp(-0.5 * up_rows * up_rows)
    return (up_rows * below).astype(BF), below + up_rows * density


def per_device(
    inputs,
    cotangent,
    block_order,
    norm_gain,
    norm_bias,
    qkv_weight,
    biases,
    out_weight,
    up_weight,
    down_weight,
):
    rows_dev = inputs.shape[2]
    core = lax.axis_index("section")
    ctx_idx = lax.axis_index("ctx")
    place = lax.axis_index("fsdp")
    ranks = lax.axis_size("ctx")
    squares = lax.axis_size("fsdp")
    group = ranks // 2
    micro = ctx_idx // group

    def rank_of(core_idx, ctx_of):
        return (ctx_of + core_idx * group) % ranks

    def places_of(rank):
        block = rows_dev // 2
        within = jnp.arange(rows_dev, dtype=jnp.int32)
        first = block_order[rank]
        block_ids = jnp.where(within < block, first, 2 * ranks - 1 - first)
        return block_ids * block + within % block

    def take_rows(whole):
        here = pick(whole[:, 0], micro)
        there = across_halves(pick(whole[:, 0], 1 - micro), 1, 1)
        return jnp.where(core == 0, here, there)

    def deliver(rows, layer):
        moved = across_halves(rows, 1, layer)
        here = rows if layer == 0 else swap_cores(rows)
        first = jnp.where(micro == 0, here, moved)
        second = jnp.where(micro == 0, moved, here)
        return jnp.stack([first, second])

    packed = jnp.concatenate([norm_gain[0].reshape(-1), norm_bias[0].reshape(-1), biases[0]])
    vectors, vectors_landed = gather_vectors(packed, core, place)
    query_own = qkv_weight[0]
    query_sib = swap_cores(query_own)
    head = tied(jnp.where(core == 0, query_own, query_sib), *vectors_landed)
    slab = down_weight.shape[1] // 4
    rest_own = jnp.concatenate(
        [up_weight[0], *[down_weight[0, j * slab : (j + 1) * slab] for j in range(4)], out_weight[0]],
        -1,
    )
    rest_own = tied(rest_own, head)
    rest_sib = swap_cores(rest_own)
    rest_first = jnp.where(core == 0, rest_own, rest_sib)
    rest_next = jnp.where(core == 1, rest_own, rest_sib)
    query_next = jnp.where(core == 1, query_own, query_sib)
    blocks = [
        head,
        rest_first,
        jnp.concatenate([query_next, rest_next[:, :FF]], -1),
        rest_next[:, FF:],
    ]
    matrices = gather_weights(blocks, core, place)
    tok_low = take_rows(inputs)
    weights = []
    for layer in (0, 1):
        vec = vectors[layer]
        width = norm_gain.shape[2]
        gains = [vec[:, j * width : (j + 1) * width].reshape(D) for j in (0, 1)]
        shifts = [vec[:, (2 + j) * width : (3 + j) * width].reshape(D) for j in (0, 1)]
        bias = vec[:, 4 * width :].reshape(-1)
        biases_of = (bias[: 3 * D], bias[3 * D : 4 * D], bias[4 * D : 4 * D + FF], bias[4 * D + FF :])
        weights.append((matrices[layer], gains, shifts, biases_of))

    own_places = places_of(rank_of(core, ctx_idx))
    key_places = jnp.concatenate(
        [places_of(rank_of(one, ctx_idx ^ j)) for one in (core, 1 - core) for j in range(group)]
    )
    ahead = rotary_tables(own_places, 1.0, 2 * LANES)
    back = rotary_tables(own_places, -1.0, LANES)
    still = (jnp.ones_like(ahead[0]), jnp.zeros_like(ahead[0]), jnp.zeros_like(ahead[0]))
    tables = [jnp.stack([ahead[k] * 0.125, ahead[k], still[k]]) for k in range(3)]
    mask = jnp.where(own_places[None, :] >= key_places[:, None], 0.0, -1e30)
    weights[0][0][0] = tied(
        weights[0][0][0], weights[0][1:], weights[1][1:], ahead, back, tables, mask
    )

    top_grad = take_rows(cotangent)
    kept = []
    layer_outs = []
    for layer in (0, 1):
        (qkv_mat, up_mat, down_mat, out_mat), gains, shifts, bias = weights[layer]
        tok_rows = tok_low.astype(F32)
        row_mean = jnp.mean(tok_rows, -1, keepdims=True)
        centred = tok_rows - row_mean
        inverse = lax.rsqrt(jnp.mean(centred * centred, -1, keepdims=True) + 1e-05)
        normed = centred * inverse
        attn_in = (normed * gains[0] + shifts[0]).astype(BF)
        mlp_in = (normed * gains[1] + shifts[1]).astype(BF)
        query, pair = qkv_rows_of(attn_in, qkv_mat, bias[0], tables)
        near = [pair, *[along_ctx(pair, j) for j in range(1, group)]]
        pairs = near + [swap_cores(one) for one in near]
        up_rows = dot_f32(mlp_in, up_mat) + bias[2]
        gelu_rows, slope = gelu_and_slope(up_rows)
        mlp_rows = dot_f32(gelu_rows, down_mat) + bias[3]
        mixed, level = attention(query, pairs, mask)
        attn_rows = dot_f32(mixed, out_mat) + bias[1]
        tok_low = (tok_rows + (attn_rows + mlp_rows)).astype(BF)
        kept.append(
            (normed, inverse, attn_in, mlp_in, query, pairs, level, mixed, slope, gelu_rows)
        )
        layer_outs.append(tok_low)

    grad_low = top_grad
    blocks = ranks * squares

    def fold(grad):
        split = grad.reshape(ranks, squares, -1, grad.shape[1])
        return [split[..., j : j + D] for j in range(0, grad.shape[1], D)]

    def enter(layer, grad_low):
        (qkv_mat, up_mat, down_mat, out_mat), gains, shifts, bias = weights[layer]
        mlp_in, slope, gelu_rows = kept[layer][3], kept[layer][8], kept[layer][9]
        down_term = dot_rows(gelu_rows, grad_low)
        up_grad = (dot_t(grad_low, down_mat) * slope).astype(BF)
        up_term = dot_rows(mlp_in, up_grad)
        wide = Reduction(
            jnp.concatenate(fold(down_term) + fold(up_term), 2), core, place, ctx_idx
        )
        return wide, up_grad, dot_t(grad_low, out_mat).astype(BF)

    remote = [n for n in range(2 * group) if n % group]

    def attend_back(layer, mixed_grad, chosen_rows, before=None):
        query, pairs, level, mixed = kept[layer][4:8]
        return attention_back(
            query, pairs, chosen_rows, mask, level, mixed, mixed_grad, back, before
        )

    def exchange(near, far):
        far = swap_cores(far)
        return [
            along_ctx((near[j].astype(F32) + far[j].astype(F32)).astype(BF), j + 1)
            for j in range(group - 1)
        ]

    def mlp_part(layer, grad_low, up_grad):
        up_mat = weights[layer][0][1]
        return dot_t(up_grad, up_mat), dot_rows(kept[layer][7], grad_low)

    def leave(layer, grad_low, qkv_grad, qkv_sums, mlp_back, up_grad):
        (qkv_mat, up_mat, down_mat, out_mat), gains, shifts, bias = weights[layer]
        normed, inverse = kept[layer][:2]
        attn_back = dot_t(qkv_grad, qkv_mat)
        norm_grad = attn_back * gains[0] + mlp_back * gains[1]
        centre = jnp.mean(norm_grad, -1, keepdims=True)
        along = jnp.mean(norm_grad * normed, -1, keepdims=True)
        back_rows = grad_low.astype(F32) + (norm_grad - centre - normed * along) * inverse
        gain_terms = [jnp.sum(attn_back * normed, 0), jnp.sum(mlp_back * normed, 0)]
        shift_terms = [jnp.sum(attn_back, 0), jnp.sum(mlp_back, 0)]
        grad_total = jnp.sum(grad_low.astype(F32), 0)
        bias_term = jnp.concatenate(
            [qkv_sums[0], grad_total, jnp.sum(up_grad.astype(F32), 0), grad_total]
        )
        small = jnp.concatenate(
            [one.reshape(blocks, -1) for one in gain_terms + shift_terms + [bias_term]], 1
        )
        small = jnp.pad(small, ((0, 0), (0, 16 * D - small.shape[1])))
        return back_rows.astype(BF), small.reshape(ranks, squares, 16, D).astype(BF)

    def reduction_of(parts):
        return Reduction(jnp.concatenate(parts, 2), core, place, ctx_idx)

    wide_1, up_grad, mixed_grad = enter(1, grad_low)
    before, near, far = attend_back(1, mixed_grad, remote)
    before, near, far, mixed_grad = settle([wide_1], before, near, far, mixed_grad)
    parts = exchange(near, far)
    wide_1.step()
    mlp_back, out_term = mlp_part(1, grad_low, up_grad)
    before, mlp_back, out_term = together(before, mlp_back, out_term)
    query_grad, near, far = attend_back(1, mixed_grad, [0, group], before)
    query_grad, near, far, mlp_back, out_term, *parts = settle(
        [wide_1], query_grad, near, far, mlp_back, out_term, *parts
    )
    parts = [near[0], swap_cores(far)[0], *parts]
    qkv_grad, qkv_sums = join_grads(query_grad, back, parts)
    low_grad, small = leave(1, grad_low, qkv_grad, qkv_sums, mlp_back, up_grad)
    qkv_term = dot_rows(kept[1][2], qkv_grad)
    thin_1 = reduction_of(fold(qkv_term) + fold(out_term) + [small])
    wide_1.step()

    wide_0, up_grad, mixed_grad = enter(0, low_grad)
    late = [deliver(low_grad, 1), *[deliver(one, j) for j, one in enumerate(layer_outs)]]
    mixed_grad, up_grad, *late = settle([thin_1, wide_1], mixed_grad, up_grad, *late)
    thin_1.step()
    wide_1.step()
    before, near, far = attend_back(0, mixed_grad, remote)
    before, near, far, mixed_grad = settle(
        [wide_0, thin_1, wide_1], before, near, far, mixed_grad
    )
    parts = exchange(near, far)
    wide_0.step()
    thin_1.step()
    mlp_back, out_term = mlp_part(0, low_grad, up_grad)
    before, mlp_back, out_term = together(before, mlp_back, out_term)
    query_grad, near, far = attend_back(0, mixed_grad, [0, group], before)
    far = swap_cores(far)
    query_term = dot_rows(kept[0][2], query_grad)
    middle = reduction_of(fold(query_term) + fold(out_term))
    query_grad, near, far, mlp_back, *parts = settle(
        [wide_0, thin_1, middle], query_grad, near, far, mlp_back, *parts
    )
    parts = [near[0], far[0], *parts]
    qkv_grad, qkv_sums = join_grads(query_grad, back, parts)
    wide_0.step()
    thin_1.step()
    middle.step()
    qkv_term = dot_rows(kept[0][2], qkv_grad[:, D:])
    last_grad, small = leave(0, low_grad, qkv_grad, qkv_sums, mlp_back, up_grad)
    thin_0 = reduction_of(fold(qkv_term) + [small])
    (first_grads,) = settle([thin_0, wide_0, thin_1, middle], deliver(last_grad, 0))
    for one in (thin_0, wide_0, middle):
        one.step()
    settle([thin_0, wide_0, middle])
    grad_outs = [first_grads, late[0]]
    layer_outs = late[1:]
    small_width = (4 * D + biases.shape[1] * squares) // blocks

    def finish(first, second):
        mine = jnp.where(core == 0, first, second)
        got = swap_cores(jnp.where(core == 0, second, first))
        return jnp.where(
            core == 0, jnp.concatenate([mine, got], -1), jnp.concatenate([got, mine], -1)
        )

    narrow = D // blocks
    middle, low_thin = middle.finish(), thin_0.finish()
    low_thin = jnp.concatenate(
        [middle[:narrow], low_thin[: 2 * narrow], middle[narrow:], low_thin[2 * narrow :]]
    )
    wide = finish(wide_0.finish(), wide_1.finish())
    thin = finish(low_thin, thin_1.finish())
    down_rows = FF // blocks

    def unfold(rows, count):
        return jnp.concatenate([rows[j * narrow : (j + 1) * narrow] for j in range(count)], -1)

    down_out = wide[:down_rows]
    up_out = unfold(wide[down_rows:], 4)
    qkv_out = unfold(thin, 3)
    out_out = thin[3 * narrow : 4 * narrow]
    small = thin[4 * narrow :].reshape(-1)[:small_width]
    gain_out = small[: 2 * narrow].reshape(2, narrow)
    shift_out = small[2 * narrow : 4 * narrow].reshape(2, narrow)
    bias_out = small[4 * narrow :]
    layer_out = jnp.where(core == 0, layer_outs[0], layer_outs[1])
    input_grads = jnp.where(core == 0, grad_outs[0], grad_outs[1])
    return (
        layer_out[None, :, None],
        input_grads[None, :, None],
        gain_out[None],
        shift_out[None],
        qkv_out[None],
        bias_out[None],
        out_out[None],
        up_out[None],
        down_out[None],
    )


def solution(mesh):
    in_specs = (
        P(None, "fsdp", "ctx", None),
        P(None, "fsdp", "ctx", None),
        P(),
        P("section", None, "fsdp"),
        P("section", None, "fsdp"),
        P("section", "fsdp", None),
        P("section", "fsdp"),
        P("section", "fsdp", None),
        P("section", "fsdp", None),
        P("section", "fsdp", None),
    )
    out_specs = (
        P("section", None, "fsdp", "ctx", None),
        P("section", None, "fsdp", "ctx", None),
        P("section", None, ("ctx", "fsdp")),
        P("section", None, ("ctx", "fsdp")),
        P("section", ("ctx", "fsdp"), None),
        P("section", ("ctx", "fsdp")),
        P("section", ("ctx", "fsdp"), None),
        P("section", ("ctx", "fsdp"), None),
        P("section", ("ctx", "fsdp"), None),
    )
    return jax.shard_map(
        per_device, mesh=mesh, in_specs=in_specs, out_specs=out_specs, check_vma=False
    )
```
